32 devices in a mesh: pas: 16 (over z, y, core), tp: 2 (over x).
Axes of the slice: x: 2, y: 2, z: 4, core: 2. Of those that a mesh axis runs over, the one named last changes fastest.
Arguments:
- passage_hidden: bfloat16 [16384, 8192], P('pas', 'tp'), may hold values from -6 to 6
- kv_weight: bfloat16 [1024, 8192], P('pas', 'tp'), may hold values from -0.0625 to 0.0625
- queries: bfloat16 [8192, 4096], P('pas', 'tp'), may hold values from -600 to 600
- query_kv: bfloat16 [8192, 1024], P('pas', 'tp'), may hold values from -6 to 6
- out_grad: bfloat16 [8192, 4096], P('pas', 'tp'), may hold values from -6 to 6
- source_device: int32 [64, 8], P('pas'), may hold values from 0 to 15, all different within a row; in each aligned block of 4 rows (0 to 3, 4 to 7, ...) at most 4 rows name the same one
- source_slot: int32 [64, 8], P('pas'), may hold values from 0 to 7
Outputs:
- query_grad: bfloat16 [8192, 4096], P('pas', 'tp')
- query_kv_grad: bfloat16 [8192, 1024], P('pas', 'tp')
- weight_grad: float32 [1024, 8192], P('pas', 'tp')
The draws below stay inside these ranges and needn't reach their ends.
Inputs may be any that keep to these rules, and one draw needn't show every extreme that they name: `source_device`: each query names 8 different owners; among the 4 queries of one index of pas no owner is named more than 4 times, and one owner exactly 4 times.
All inputs are finite; a program needn't handle non-finite values.
Results may differ from the reference program's by a relative error of at most 0.0095.
Values may be sent and summed in bfloat16 or wider, within the bound.
A program may use at most 128 MiB of HBM per device.

```python
import math
import jax
import jax.numpy as jnp
import numpy as np
from jax import lax

D = 8192
HD = 128
PLEN = 128
PAS_DEV = 8
Q_DEV = 4
QLEN = 128
TOPR = 8
OWNERS = 16
CAP = 4
PASSAGES = 128
QUERIES = 64
QH = 32
KVW = 1024


def shared_pairs(key):
    values = jax.random.normal(key, (QUERIES * QLEN, KVW), jnp.float32)
    return jnp.clip(values, -6.0, 6.0).astype(jnp.bfloat16).astype(jnp.float32)


def draw_query_kv(key, part):
    pairs = shared_pairs(key)
    return pairs.astype(jnp.bfloat16)


def draw_queries(key, part):
    key = jax.random.fold_in(key, 11)
    base = jax.random.normal(key, (QUERIES * QLEN, QH * HD), jnp.float32)
    return jnp.clip(base, -600.0, 600.0).astype(jnp.bfloat16)


def plant(drawn, stream_key, least, top_value):
    longest = drawn.shape.index(max(drawn.shape))
    spots = []
    for shift in (0, 1):
        where = [jax.random.randint(jax.random.fold_in(stream_key, axis), (), 0, length) for axis, length in enumerate(drawn.shape)]
        where[longest] = (where[longest] + shift) % drawn.shape[longest]
        spots.append(tuple(where))
    return drawn.at[spots[0]].set(least).at[spots[1]].set(top_value)


def block_levels(own_key, extent, cuts, least, high):
    def one(position, blocks):
        steps = jax.random.uniform(jax.random.fold_in(jax.random.fold_in(own_key, 6), position), (blocks,), jnp.float32, least / len(cuts), high / len(cuts))
        return jnp.repeat(jnp.exp(steps), extent[position] // blocks).reshape((-1,) + (1,) * (len(extent) - position - 1))

    loudness = one(*cuts[0])
    for cut in cuts[1:]:
        loudness = loudness * one(*cut)
    return loudness


def routed_block(stream_key, own, number, rows, count, top, bound, slope):
    ranking = jax.random.permutation(stream_key, count)
    heavy_load, usual = load_shares(count, rows * top, bound, slope, True), load_shares(count, rows * top, bound, slope, False)
    places = jnp.arange(count)

    def named(sizes, offset_by):
        used = int((sizes > 0).sum())
        fixed = max(1, used // 4)
        passed = fixed + (places - fixed + offset_by * (used - fixed)) % max(1, count - fixed)
        return jnp.zeros((count,), jnp.int32).at[ranking[jnp.where(places < fixed, places, passed)]].set(jnp.asarray(sizes, jnp.int32))

    sizes = jnp.where(number % 4 == 0, named(heavy_load, number // 4), named(usual, number - number // 4 - 1))
    mixed = jax.random.permutation(jax.random.fold_in(own, 3), count)
    source_of, sink = mixed[0:count // 2 * 2:2], mixed[1:count // 2 * 2:2]
    margin = jnp.minimum(sizes[source_of] - 1, bound - sizes[sink]) // 2
    margin = jnp.where((source_of == ranking[0]) | (sink == ranking[0]) | (sizes[sink] == 0), 0, jnp.maximum(margin, 0))
    passed = jax.random.randint(jax.random.fold_in(own, 4), (count // 2,), 0, 1 << 20) % (margin + 1)
    sizes = sizes.at[source_of].add(-passed).at[sink].add(passed)
    members = jnp.searchsorted(jnp.cumsum(sizes), jnp.arange(rows * top), side="right").astype(jnp.int32)
    listing = members.reshape(top, rows).T
    listing = listing[jax.random.permutation(jax.random.fold_in(own, 1), rows)]
    offset_by = jax.random.randint(jax.random.fold_in(own, 2), (rows, 1), 0, top)
    return jnp.take_along_axis(listing, (jnp.arange(top)[None, :] + offset_by) % top, axis=1)


def load_shares(amount, total, reach, lean, full):
    loads = [(1 << 20) // math.isqrt(grade ** lean) + 1 for grade in range(1, amount + 1)]
    largest = reach if full else min(reach, max(-(-total // amount), total * loads[0] // sum(loads)))
    least = 1 if total - largest >= amount - 1 else 0
    counts, rest = [largest] + [least] * (amount - 1), total - largest - least * (amount - 1)
    while rest > 0:
        candidates = [i for i in range(1, amount) if counts[i] < largest] or [i for i in range(1, amount) if counts[i] < reach]
        mass, remaining = sum([loads[i] for i in candidates]), rest
        for i in candidates:
            more = min(reach - counts[i], max(1, remaining * loads[i] // mass), rest)
            counts[i] = counts[i] + more
            rest = rest - more
    return np.array(counts)


def gaussian(own_key, extent, scale, bound, shards=(), held_as=jnp.bfloat16):
    values = scale * jax.random.normal(own_key, extent, jnp.float32)
    if shards:
        values = values * block_levels(own_key, extent, shards, -0.22, 0.18)
    return jnp.clip(values, -bound, bound).astype(held_as)


def setup_inputs(seed: int = 0) -> dict:
    arg_keys = jax.random.split(jax.random.key(seed), 8)
    passage_hidden = gaussian(arg_keys[0], (PASSAGES * PLEN, D), 1.0, 6.0, ((0, 16), (1, 2)))
    kv_weight = gaussian(arg_keys[1], (KVW, D), D ** -0.5, 0.0625, ((0, 16), (1, 2)))
    queries = draw_queries(jax.random.fold_in(arg_keys[7], 71), 0)
    query_kv = draw_query_kv(jax.random.fold_in(arg_keys[7], 71), 0)
    out_grad = gaussian(arg_keys[4], (QUERIES * QLEN, QH * HD), 1.0, 6.0, ((0, 16), (1, 2)))
    source_device_keys = jax.random.split(jax.random.fold_in(arg_keys[5], 1), QUERIES // Q_DEV)
    source_device_turns = jax.random.permutation(jax.random.fold_in(arg_keys[5], 3), QUERIES // Q_DEV)
    source_device = jax.vmap(lambda own, number: routed_block(jax.random.fold_in(arg_keys[5], 2), own, number, Q_DEV, OWNERS, TOPR, CAP, 2))(source_device_keys, source_device_turns).reshape((QUERIES, TOPR))
    source_slot = plant(jax.random.randint(arg_keys[6], (QUERIES, TOPR), 0, PAS_DEV), jax.random.fold_in(arg_keys[6], 1), 0, PAS_DEV - 1).astype(jnp.int32)
    return {"passage_hidden": passage_hidden, "kv_weight": kv_weight, "queries": queries, "query_kv": query_kv, "out_grad": out_grad, "source_device": source_device, "source_slot": source_slot}


def attend_block(query_rows, keys_values, grad_out, prefix):
    highest = lax.Precision.HIGHEST
    query_len = query_rows.shape[0]
    key_len = keys_values.shape[0]
    kv_heads = keys_values.shape[1] // (2 * HD)
    group_size = query_rows.shape[1] // (HD * kv_heads)
    paired = keys_values.astype(jnp.float32).reshape(key_len, kv_heads, 2, HD)
    key_heads = paired[:, :, 0, :]
    value_heads = paired[:, :, 1, :]
    query_heads = query_rows.astype(jnp.float32).reshape(query_len, kv_heads, group_size, HD)
    grad_heads = grad_out.astype(jnp.float32).reshape(query_len, kv_heads, group_size, HD)
    scaling = HD ** -0.5
    scores = jnp.einsum('qhgd,khd->hgqk', query_heads, key_heads, precision=highest) * scaling
    row_index = jnp.arange(query_len)[:, None]
    col_index = jnp.arange(key_len)[None, :]
    visible = jnp.logical_or(col_index < prefix, col_index - prefix <= row_index)
    scores = jnp.where(visible, scores, jnp.float32(-1e30))
    largest = jnp.max(scores, axis=-1, keepdims=True)
    exponent = jnp.exp(scores - largest)
    weights = exponent / jnp.sum(exponent, axis=-1, keepdims=True)
    weights_low = lax.optimization_barrier(weights.astype(jnp.bfloat16)).astype(jnp.float32)
    outputs = jnp.einsum('hgqk,khd->hgqd', weights_low, value_heads, precision=highest)
    delta_rows = jnp.sum(outputs * grad_heads.transpose(1, 2, 0, 3), axis=-1, keepdims=True)
    grad_weights = jnp.einsum('qhgd,khd->hgqk', grad_heads, value_heads, precision=highest)
    grad_scores = weights * (grad_weights - delta_rows)
    grad_low = lax.optimization_barrier(grad_scores.astype(jnp.bfloat16)).astype(jnp.float32)
    grad_query = jnp.einsum('hgqk,khd->qhgd', grad_low, key_heads, precision=highest) * scaling
    grad_query = grad_query.astype(jnp.bfloat16).reshape(query_len, kv_heads * group_size * HD)
    grad_keys = jnp.einsum('hgqk,qhgd->khd', grad_low, query_heads, precision=highest) * scaling
    grad_values = jnp.einsum('hgqk,qhgd->khd', weights_low, grad_heads, precision=highest)
    grad_pairs = jnp.stack([grad_keys, grad_values], axis=2).reshape(key_len, kv_heads * 2 * HD)
    return grad_query, grad_pairs


def reference(passage_hidden, kv_weight, queries, query_kv, out_grad, source_device, source_slot):
    width = kv_weight.shape[0]
    projected = jnp.dot(passage_hidden, kv_weight.T, preferred_element_type=jnp.float32).astype(jnp.bfloat16)
    passage_kv = projected.reshape(PASSAGES, PLEN, width)
    passage_ids = (source_device * PAS_DEV + source_slot).astype(jnp.int32)
    remote_rows = TOPR * PLEN

    def one_query(grad_total, inputs):
        query_rows, own_pairs, grad_out, chosen = inputs
        fetched = passage_kv[chosen].reshape(remote_rows, width)
        keys_values = jnp.concatenate([fetched, own_pairs], axis=0)
        grad_query, grad_pairs = attend_block(query_rows, keys_values, grad_out, remote_rows)
        remote_grad = lax.optimization_barrier(grad_pairs[:remote_rows].astype(jnp.bfloat16))
        remote_grad = remote_grad.astype(jnp.float32).reshape(TOPR, PLEN, width)
        grad_total = grad_total.at[chosen].add(remote_grad)
        own_grad = grad_pairs[remote_rows:].astype(jnp.bfloat16)
        return grad_total, (grad_query, own_grad)

    initial = jnp.zeros((PASSAGES, PLEN, width), jnp.float32)
    inputs = (queries.reshape(QUERIES, QLEN, queries.shape[1]),
              query_kv.reshape(QUERIES, QLEN, width),
              out_grad.reshape(QUERIES, QLEN, out_grad.shape[1]),
              passage_ids)
    grad_total, (grad_queries, own_grads) = lax.scan(one_query, initial, inputs)
    grad_kv = grad_total.astype(jnp.bfloat16).reshape(PASSAGES * PLEN, width)
    weight_grad = jnp.dot(grad_kv.T, passage_hidden, preferred_element_type=jnp.float32)
    return (grad_queries.reshape(QUERIES * QLEN, queries.shape[1]),
            own_grads.reshape(QUERIES * QLEN, width),
            weight_grad)
```

```python
import functools
import math
import jax
import jax.numpy as jnp
from jax import lax
from jax.experimental import pallas as pl
from jax.experimental.pallas import tpu as pltpu
from jax.sharding import PartitionSpec as P

HD = 128
PLEN = 128
MIB = 1 << 20


def ring_place(chips):
    me = lax.axis_index("pas")
    core = lax.rem(me, 2)
    chip = lax.div(me, 2)
    side = lax.rem(chip, 2)
    deep = lax.div(chip, 2)
    place = deep + side * (chips - 1 - 2 * deep)

    def chip_at(position):
        q = lax.rem(position + 2 * chips, chips)
        half = lax.div(q, chips // 2)
        return 2 * q + half * (2 * chips - 1 - 4 * q)

    return core, place, chip_at


def greet(others):
    barrier = pltpu.get_barrier_semaphore()
    for other in others:
        pl.semaphore_signal(
            barrier, inc=1, device_id={"pas": other}, device_id_type=pl.DeviceIdType.MESH
        )
    pl.semaphore_wait(barrier, len(others))


def send(src, dst, send_sem, recv_sem, other):
    return pltpu.make_async_remote_copy(
        src_ref=src,
        dst_ref=dst,
        send_sem=send_sem,
        recv_sem=recv_sem,
        device_id={"pas": other},
        device_id_type=pl.DeviceIdType.MESH,
    )


def gather_kernel(chips, lanes, x_ref, out_ref, own_sem, ring_send, ring_recv, pair_send, pair_recv):
    core, place, chip_at = ring_place(chips)
    mine = chip_at(place)
    partner = 2 * mine + 1 - core
    nexts = (2 * chip_at(place + 1) + core, 2 * chip_at(place - 1) + core)
    greet((nexts[0], nexts[1], partner))
    rings, pairs = {}, []
    for step in range(chips):
        for lane in range(lanes):
            for way in range(2):
                back = step if way == 0 else -step
                where = chip_at(place - back)
                slot = out_ref.at[where, core, way, lane]
                if step == 0:
                    src = x_ref.at[way, lane]
                else:
                    rings[step - 1, way, lane].wait_recv()
                    src = slot
                if step < chips - 1:
                    copy = send(
                        src, slot, ring_send.at[step, way, lane], ring_recv.at[step, way, lane], nexts[way]
                    )
                    copy.start()
                    rings[step, way, lane] = copy
                copy = send(
                    src, slot, pair_send.at[step, way, lane], pair_recv.at[step, way, lane], partner
                )
                copy.start()
                pairs.append(copy)
        if step == 0:
            own = pltpu.make_async_copy(x_ref, out_ref.at[mine, core], own_sem)
            own.start()
    own.wait()
    for copy in rings.values():
        copy.wait_send()
    for copy in pairs:
        copy.wait()


def ring_gather(x, chips, collective_id):
    rows, width = x.shape
    lanes = 2 if rows % 64 == 0 else 1
    high = rows // (2 * lanes)
    out = pl.pallas_call(
        functools.partial(gather_kernel, chips, lanes),
        out_shape=jax.ShapeDtypeStruct((chips, 2, 2, lanes, high, width), x.dtype),
        in_specs=[pl.BlockSpec(memory_space=pl.ANY)],
        out_specs=pl.BlockSpec(memory_space=pl.ANY),
        scratch_shapes=[
            pltpu.SemaphoreType.DMA,
            pltpu.SemaphoreType.DMA((chips, 2, lanes)),
            pltpu.SemaphoreType.DMA((chips, 2, lanes)),
            pltpu.SemaphoreType.DMA((chips, 2, lanes)),
            pltpu.SemaphoreType.DMA((chips, 2, lanes)),
        ],
        compiler_params=pltpu.CompilerParams(collective_id=collective_id, has_side_effects=True),
    )(x.reshape(2, lanes, high, width))
    return out.reshape(chips * 2 * rows, width)


def sum_kernel(
    chips, lanes, x_ref, out_ref, mine, pair, got,
    own_sem, pair_send, pair_recv, ring_send, ring_recv,
):
    core, place, chip_at = ring_place(chips)
    partner = 2 * chip_at(place) + 1 - core
    nexts = (2 * chip_at(place + 1) + core, 2 * chip_at(place - 1) + core)
    high = x_ref.shape[4]
    part = 16
    owns, pairs, rings = {}, {}, {}
    greet((nexts[0], nexts[1], partner))
    for step in range(chips):
        for way in range(2):
            ahead = place - 1 - step if way == 0 else place + 1 + step
            where = chip_at(ahead)
            copy = send(
                x_ref.at[where, 1 - core, way],
                pair.at[way, step],
                pair_send.at[way, step],
                pair_recv.at[way, step],
                partner,
            )
            copy.start()
            pairs[way, step] = copy
            copy = pltpu.make_async_copy(
                x_ref.at[where, core, way], mine.at[way, step], own_sem.at[way, step]
            )
            copy.start()
            owns[way, step] = copy
    for step in range(chips):
        last = step == chips - 1
        for lane in range(lanes):
            for way in range(2):
                if lane == 0:
                    owns[way, step].wait()
                    pairs[way, step].wait_recv()
                if step > 0:
                    rings[step - 1, way, lane].wait_recv()

                def add(index, carry, way=way, lane=lane):
                    here = pl.ds(pl.multiple_of(index * part, part), part)
                    total = mine[way, step, lane, here, :].astype(jnp.float32)
                    total += pair[way, step, lane, here, :].astype(jnp.float32)
                    if step > 0:
                        total += got[way, step - 1, lane, here, :].astype(jnp.float32)
                    if last:
                        out_ref[way, lane, here, :] = total.astype(out_ref.dtype)
                    else:
                        mine[way, step, lane, here, :] = total.astype(mine.dtype)
                    return carry

                lax.fori_loop(0, high // part, add, 0)
                if not last:
                    copy = send(
                        mine.at[way, step, lane],
                        got.at[way, step, lane],
                        ring_send.at[step, way, lane],
                        ring_recv.at[step, way, lane],
                        nexts[way],
                    )
                    copy.start()
                    rings[step, way, lane] = copy
    for copy in pairs.values():
        copy.wait_send()
    for copy in rings.values():
        copy.wait_send()


def ring_sum(x, chips, collective_id, out_dtype):
    rows, width = x.shape
    rows = rows // (2 * chips)
    lanes = 2 if rows % 64 == 0 else 1
    high = rows // (2 * lanes)
    block = (lanes, high, width)
    out = pl.pallas_call(
        functools.partial(sum_kernel, chips, lanes),
        out_shape=jax.ShapeDtypeStruct((2,) + block, out_dtype),
        in_specs=[pl.BlockSpec(memory_space=pl.ANY)],
        out_specs=pl.BlockSpec(memory_space=pltpu.VMEM),
        scratch_shapes=[
            pltpu.VMEM((2, chips) + block, x.dtype),
            pltpu.VMEM((2, chips) + block, x.dtype),
            pltpu.VMEM((2, chips) + block, x.dtype),
            pltpu.SemaphoreType.DMA((2, chips)),
            pltpu.SemaphoreType.DMA((2, chips)),
            pltpu.SemaphoreType.DMA((2, chips)),
            pltpu.SemaphoreType.DMA((chips, 2, lanes)),
            pltpu.SemaphoreType.DMA((chips, 2, lanes)),
        ],
        compiler_params=pltpu.CompilerParams(
            collective_id=collective_id, has_side_effects=True, vmem_limit_bytes=48 * MIB
        ),
    )(x.reshape((chips, 2, 2) + block))
    return out.reshape(rows, width)


def attend_kernel(group, retrieved, ids_ref, q_ref, g_ref, own_ref, *refs):
    passages = refs[:retrieved]
    dq_ref, remote_ref, down_ref, keys, values, dkeys, dvalues = refs[retrieved:]
    scaling = HD ** (-0.5)
    remote = retrieved * PLEN
    tokens = q_ref.shape[0]
    for i in range(retrieved):
        keys[i * PLEN : (i + 1) * PLEN, :] = passages[i][0, :, :HD]
        values[i * PLEN : (i + 1) * PLEN, :] = passages[i][0, :, HD:]
    keys[remote:, :] = own_ref[:, :HD]
    values[remote:, :] = own_ref[:, HD:]
    row = lax.broadcasted_iota(jnp.int32, (2 * tokens, tokens), 0)
    col = lax.broadcasted_iota(jnp.int32, (2 * tokens, tokens), 1)
    hidden = col > jnp.where(row >= tokens, row - tokens, row)

    def dot(a, b, dims):
        return lax.dot_general(a, b, ((dims[0], dims[1]), ((), ())), preferred_element_type=jnp.float32)

    for pair in range(group // 2):
        lo, mid, hi = 2 * pair * HD, (2 * pair + 1) * HD, (2 * pair + 2) * HD
        q = jnp.concatenate([q_ref[:, lo:mid], q_ref[:, mid:hi]], axis=0)
        g = jnp.concatenate([g_ref[:, lo:mid], g_ref[:, mid:hi]], axis=0)
        k, v = keys[...], values[...]
        scores = dot(q, k, ((1,), (1,)))
        tail = jnp.where(hidden, jnp.float32(-1e30), scores[:, remote:])
        scores = jnp.concatenate([scores[:, :remote], tail], axis=1)
        largest = jnp.max(scores, axis=1, keepdims=True)
        exponent = jnp.exp2((scores - largest) * jnp.float32(scaling * math.log2(math.e)))
        weights = exponent * (1.0 / jnp.sum(exponent, axis=1, keepdims=True))
        low = weights.astype(jnp.bfloat16)
        outputs = dot(low, v, ((1,), (0,)))
        delta = jnp.sum(outputs * g.astype(jnp.float32), axis=1, keepdims=True)
        grad = (weights * (dot(g, v, ((1,), (1,))) - delta)).astype(jnp.bfloat16)
        dq = (dot(grad, k, ((1,), (0,))) * scaling).astype(dq_ref.dtype)
        dq_ref[:, lo:mid] = dq[:tokens]
        dq_ref[:, mid:hi] = dq[tokens:]
        dk = dot(grad, q, ((0,), (0,)))
        dv = dot(low, g, ((0,), (0,)))
        if pair == 0:
            dkeys[...] = dk
            dvalues[...] = dv
        else:
            dkeys[...] += dk
            dvalues[...] += dv
    for i in range(retrieved):
        remote_ref[i, :, :HD] = (dkeys[i * PLEN : (i + 1) * PLEN, :] * scaling).astype(remote_ref.dtype)
        remote_ref[i, :, HD:] = dvalues[i * PLEN : (i + 1) * PLEN, :].astype(remote_ref.dtype)
    down_ref[:, :HD] = (dkeys[remote:, :] * scaling).astype(down_ref.dtype)
    down_ref[:, HD:] = dvalues[remote:, :].astype(down_ref.dtype)


def attend(ids, queries, out_grad, query_kv, passage_kv, queries_here, retrieved):
    tokens = queries.shape[0] // queries_here
    width = query_kv.shape[1]
    heads = width // (2 * HD)
    wide = queries.shape[1] // heads
    group = wide // HD
    keys = retrieved * PLEN + tokens

    def passage_spec(i):
        return pl.BlockSpec((1, PLEN, 2 * HD), lambda n, h, ids: (ids[n * retrieved + i], 0, h))

    wide_spec = pl.BlockSpec((tokens, wide), lambda n, h, ids: (n, h))
    own_spec = pl.BlockSpec((tokens, 2 * HD), lambda n, h, ids: (n, h))
    flops = 12 * queries_here * heads * group * tokens * keys * HD
    return pl.pallas_call(
        functools.partial(attend_kernel, group, retrieved),
        grid_spec=pltpu.PrefetchScalarGridSpec(
            num_scalar_prefetch=1,
            grid=(queries_here, heads),
            in_specs=[wide_spec, wide_spec, own_spec] + [passage_spec(i) for i in range(retrieved)],
            out_specs=[
                wide_spec,
                pl.BlockSpec((retrieved, PLEN, 2 * HD), lambda n, h, ids: (n, 0, h)),
                own_spec,
            ],
            scratch_shapes=[
                pltpu.VMEM((keys, HD), jnp.bfloat16),
                pltpu.VMEM((keys, HD), jnp.bfloat16),
                pltpu.VMEM((keys, HD), jnp.float32),
                pltpu.VMEM((keys, HD), jnp.float32),
            ],
        ),
        out_shape=[
            jax.ShapeDtypeStruct(queries.shape, jnp.bfloat16),
            jax.ShapeDtypeStruct((queries_here * retrieved, PLEN, width), jnp.bfloat16),
            jax.ShapeDtypeStruct(query_kv.shape, jnp.bfloat16),
        ],
        compiler_params=pltpu.CompilerParams(vmem_limit_bytes=48 * MIB),
        cost_estimate=pl.CostEstimate(flops=flops, bytes_accessed=16 * MIB, transcendentals=0),
    )(ids, queries, out_grad, query_kv, *([passage_kv] * retrieved))


def per_device(passage_hidden, kv_weight, queries, query_kv, out_grad, source_device, source_slot):
    owners = lax.axis_size("pas")
    shares = lax.axis_size("tp")
    share = lax.axis_index("tp")
    chips = owners // 2
    rows_local = passage_hidden.shape[0]
    local_width = query_kv.shape[1]
    passages_here = rows_local // PLEN
    queries_here, retrieved = source_device.shape
    weight = ring_gather(kv_weight, chips, 0)

    def project(target):
        rows = lax.dynamic_slice_in_dim(weight, target * local_width, local_width, axis=0)
        return lax.dot_general(
            passage_hidden, rows, (((1,), (1,)), ((), ())), preferred_element_type=jnp.float32
        )

    arrived = []
    for k in range(1, shares):
        route = [(i, (i + k) % shares) for i in range(shares)]
        arrived.append(lax.ppermute(project(lax.rem(share + k, shares)), "tp", route))
    projected = project(share)
    for block in arrived:
        projected = projected + block
    passage_kv = ring_gather(projected.astype(jnp.bfloat16), chips, 1)
    passage_kv = passage_kv.reshape(owners * passages_here, PLEN, local_width)
    ids = (source_device * passages_here + source_slot).reshape(-1)
    grad_queries, remote_grads, own_grads = attend(
        ids, queries, out_grad, query_kv, passage_kv, queries_here, retrieved
    )
    chosen = (ids[:, None] == jnp.arange(owners * passages_here, dtype=jnp.int32)[None, :]).astype(
        jnp.bfloat16
    )
    dense = jnp.einsum("ep,exk->pxk", chosen, remote_grads, preferred_element_type=jnp.float32)
    dense = dense.astype(jnp.bfloat16).reshape(owners * rows_local, local_width)
    grad_kv = ring_sum(dense, chips, 2, jnp.bfloat16)
    full = jnp.zeros((rows_local, shares * local_width), jnp.bfloat16)
    full = lax.dynamic_update_slice_in_dim(full, grad_kv, share * local_width, axis=1)
    for k in range(1, shares):
        route = [(i, (i + k) % shares) for i in range(shares)]
        block = lax.ppermute(grad_kv, "tp", route)
        origin = lax.rem(share + shares - k, shares)
        full = lax.dynamic_update_slice_in_dim(full, block, origin * local_width, axis=1)
    partial = jnp.einsum("rc,rd->cd", full, passage_hidden, preferred_element_type=jnp.float32)
    weight_grad = ring_sum(partial.astype(jnp.bfloat16), chips, 3, jnp.float32)
    return grad_queries, own_grads, weight_grad


def solution(mesh):
    in_specs = (
        P("pas", "tp"),
        P("pas", "tp"),
        P("pas", "tp"),
        P("pas", "tp"),
        P("pas", "tp"),
        P("pas", None),
        P("pas", None),
    )
    out_specs = (P("pas", "tp"), P("pas", "tp"), P("pas", "tp"))
    return jax.shard_map(
        per_device, mesh=mesh, in_specs=in_specs, out_specs=out_specs, check_vma=False
    )
```

```python
import functools
import math
import jax
import jax.numpy as jnp
from jax import lax
from jax.experimental import pallas as pl
from jax.experimental.pallas import tpu as pltpu
from jax.sharding import PartitionSpec as P

HD = 128
PLEN = 128
MIB = 1 << 20


def ring_place(chips):
    me = lax.axis_index("pas")
    core = lax.rem(me, 2)
    chip = lax.div(me, 2)
    side = lax.rem(chip, 2)
    deep = lax.div(chip, 2)
    place = deep + side * (chips - 1 - 2 * deep)

    def chip_at(position):
        q = lax.rem(position + 2 * chips, chips)
        half = lax.div(q, chips // 2)
        return 2 * q + half * (2 * chips - 1 - 4 * q)

    return core, place, chip_at


def greet(others, shares=()):
    barrier = pltpu.get_barrier_semaphore()
    for place in [{"pas": other} for other in others] + [{"tp": other} for other in shares]:
        pl.semaphore_signal(barrier, inc=1, device_id=place, device_id_type=pl.DeviceIdType.MESH)
    pl.semaphore_wait(barrier, len(others) + len(shares))


def send(src, dst, send_sem, recv_sem, other, axis="pas"):
    return pltpu.make_async_remote_copy(
        src_ref=src,
        dst_ref=dst,
        send_sem=send_sem,
        recv_sem=recv_sem,
        device_id={axis: other},
        device_id_type=pl.DeviceIdType.MESH,
    )


def gather_kernel(chips, lanes, x_ref, out_ref, own_sem, ring_send, ring_recv, pair_send, pair_recv):
    core, place, chip_at = ring_place(chips)
    mine = chip_at(place)
    partner = 2 * mine + 1 - core
    nexts = (2 * chip_at(place + 1) + core, 2 * chip_at(place - 1) + core)
    greet((nexts[0], nexts[1], partner))
    rings, pairs = {}, []
    for step in range(chips):
        for lane in range(lanes):
            for way in range(2):
                back = step if way == 0 else -step
                where = chip_at(place - back)
                slot = out_ref.at[where, core, way, lane]
                if step == 0:
                    src = x_ref.at[way, lane]
                else:
                    rings[step - 1, way, lane].wait_recv()
                    src = slot
                if step < chips - 1:
                    copy = send(
                        src, slot, ring_send.at[step, way, lane], ring_recv.at[step, way, lane], nexts[way]
                    )
                    copy.start()
                    rings[step, way, lane] = copy
                copy = send(
                    src, slot, pair_send.at[step, way, lane], pair_recv.at[step, way, lane], partner
                )
                copy.start()
                pairs.append(copy)
        if step == 0:
            own = pltpu.make_async_copy(x_ref, out_ref.at[mine, core], own_sem)
            own.start()
    own.wait()
    for copy in rings.values():
        copy.wait_send()
    for copy in pairs:
        copy.wait()


def ring_gather(x, chips, collective_id):
    rows, width = x.shape
    lanes = 2 if rows % 64 == 0 else 1
    high = rows // (2 * lanes)
    out = pl.pallas_call(
        functools.partial(gather_kernel, chips, lanes),
        out_shape=jax.ShapeDtypeStruct((chips, 2, 2, lanes, high, width), x.dtype),
        in_specs=[pl.BlockSpec(memory_space=pl.ANY)],
        out_specs=pl.BlockSpec(memory_space=pl.ANY),
        scratch_shapes=[
            pltpu.SemaphoreType.DMA,
            pltpu.SemaphoreType.DMA((chips, 2, lanes)),
            pltpu.SemaphoreType.DMA((chips, 2, lanes)),
            pltpu.SemaphoreType.DMA((chips, 2, lanes)),
            pltpu.SemaphoreType.DMA((chips, 2, lanes)),
        ],
        compiler_params=pltpu.CompilerParams(collective_id=collective_id, has_side_effects=True),
    )(x.reshape(2, lanes, high, width))
    return out.reshape(chips * 2 * rows, width)


def project_kernel(
    chips, shares, lanes, hidden_ref, x_ref, out_ref, hidden, weight, joined, part, got,
    own_sem, hidden_sem, ring_send, ring_recv, pair_send, pair_recv, share_send, share_recv,
):
    core, place, chip_at = ring_place(chips)
    share = lax.axis_index("tp")
    mine = chip_at(place)
    partner = 2 * mine + 1 - core
    nexts = (2 * chip_at(place + 1) + core, 2 * chip_at(place - 1) + core)
    load = pltpu.make_async_copy(hidden_ref, hidden, hidden_sem)
    load.start()
    own = pltpu.make_async_copy(x_ref, weight.at[mine, core], own_sem)
    own.start()
    greet(
        (nexts[0], nexts[1], partner),
        [lax.rem(share + k, shares) for k in range(1, shares)],
    )
    rows = hidden.shape[0]
    tile = min(256, rows)
    half = part.shape[2]
    each = half // 2
    group = chips // shares
    rings, pairs = {}, {}

    def chip_of(step, way):
        return chip_at(place - step if way == 0 else place + step)

    def goal(step, way):
        return lax.div(chip_of(step, way), group)

    def share_copy(step, way):
        target = goal(step, way)
        slot = lax.rem(target - share + 2 * shares - 1, shares)
        slot = lax.rem(slot, shares - 1)
        return send(
            part.at[way, step],
            got.at[slot, way, step],
            share_send.at[way, step],
            share_recv.at[slot, way, step],
            target,
            "tp",
        )

    def multiply(step):
        for way in range(2):
            for lane in range(lanes):
                pairs[step, way, lane].wait_recv()
            piece = weight[chip_of(step, way), :, way]
            joined[way * half : (way + 1) * half, :] = piece.reshape(half, piece.shape[-1])

        def one(index, carry):
            here = pl.ds(pl.multiple_of(index * tile, tile), tile)
            product = lax.dot_general(
                joined[...], hidden[here, :], (((1,), (1,)), ((), ())),
                preferred_element_type=jnp.float32,
            )
            part[0, step, :, here] = product[:half]
            part[1, step, :, here] = product[half:]
            return carry

        lax.fori_loop(0, rows // tile, one, 0)
        for way in range(2):

            @pl.when(goal(step, way) != share)
            def _(way=way):
                share_copy(step, way).start()

    for step in range(chips):
        for lane in range(lanes):
            for way in range(2):
                slot = weight.at[chip_of(step, way), core, way, lane]
                if step == 0:
                    src = x_ref.at[way, lane]
                else:
                    rings[step - 1, way, lane].wait_recv()
                    src = slot
                if step < chips - 1:
                    copy = send(
                        src, slot, ring_send.at[step, way, lane], ring_recv.at[step, way, lane], nexts[way]
                    )
                    copy.start()
                    rings[step, way, lane] = copy
                copy = send(
                    src, slot, pair_send.at[step, way, lane], pair_recv.at[step, way, lane], partner
                )
                copy.start()
                pairs[step, way, lane] = copy
        if step == 0:
            load.wait()
            own.wait()
        else:
            multiply(step - 1)
    multiply(chips - 1)
    for step in range(chips):
        for way in range(2):

            @pl.when(goal(step, way) == share)
            def _(step=step, way=way):
                total = part[way, step]
                for slot in range(shares - 1):
                    send(
                        part.at[way, step],
                        got.at[slot, way, step],
                        share_send.at[way, step],
                        share_recv.at[slot, way, step],
                        lax.rem(share + 1, shares),
                        "tp",
                    ).wait_recv()
                    total = total + got[slot, way, step]
                total = total.astype(out_ref.dtype)
                where = lax.rem(chip_of(step, way), group)
                out_ref[where, 0, way] = total[:each]
                out_ref[where, 1, way] = total[each:]

            @pl.when(goal(step, way) != share)
            def _(step=step, way=way):
                share_copy(step, way).wait_send()

    for copy in rings.values():
        copy.wait_send()
    for copy in pairs.values():
        copy.wait_send()


def project(hidden, kv_weight, chips, shares, collective_id):
    rows, width = hidden.shape
    high = kv_weight.shape[0]
    lanes = 2 if high % 64 == 0 else 1
    high = high // (2 * lanes)
    half = 2 * lanes * high
    group = chips // shares
    step_sems = pltpu.SemaphoreType.DMA((chips, 2, lanes))
    out = pl.pallas_call(
        functools.partial(project_kernel, chips, shares, lanes),
        out_shape=jax.ShapeDtypeStruct((group, 2, 2, lanes * high, rows), jnp.bfloat16),
        in_specs=[pl.BlockSpec(memory_space=pl.ANY)] * 2,
        out_specs=pl.BlockSpec(memory_space=pltpu.VMEM),
        scratch_shapes=[
            pltpu.VMEM((rows, width), hidden.dtype),
            pltpu.VMEM((chips, 2, 2, lanes, high, width), kv_weight.dtype),
            pltpu.VMEM((2 * half, width), kv_weight.dtype),
            pltpu.VMEM((2, chips, half, rows), jnp.float32),
            pltpu.VMEM((shares - 1, 2, chips, half, rows), jnp.float32),
            pltpu.SemaphoreType.DMA,
            pltpu.SemaphoreType.DMA,
            step_sems,
            step_sems,
            step_sems,
            step_sems,
            pltpu.SemaphoreType.DMA((2, chips)),
            pltpu.SemaphoreType.DMA((shares - 1, 2, chips)),
        ],
        compiler_params=pltpu.CompilerParams(
            collective_id=collective_id, has_side_effects=True, vmem_limit_bytes=56 * MIB
        ),
    )(hidden, kv_weight.reshape(2, lanes, high, width))
    return out.reshape(group * 2 * 2 * lanes * high, rows).T


def sum_kernel(
    chips, lanes, x_ref, out_ref, mine, pair, got,
    own_sem, pair_send, pair_recv, ring_send, ring_recv,
):
    core, place, chip_at = ring_place(chips)
    partner = 2 * chip_at(place) + 1 - core
    nexts = (2 * chip_at(place + 1) + core, 2 * chip_at(place - 1) + core)
    high = x_ref.shape[4]
    part = 16
    owns, pairs, rings = {}, {}, {}
    greet((nexts[0], nexts[1], partner))
    for step in range(chips):
        for way in range(2):
            ahead = place - 1 - step if way == 0 else place + 1 + step
            where = chip_at(ahead)
            copy = send(
                x_ref.at[where, 1 - core, way],
                pair.at[way, step],
                pair_send.at[way, step],
                pair_recv.at[way, step],
                partner,
            )
            copy.start()
            pairs[way, step] = copy
            copy = pltpu.make_async_copy(
                x_ref.at[where, core, way], mine.at[way, step], own_sem.at[way, step]
            )
            copy.start()
            owns[way, step] = copy
    for step in range(chips):
        last = step == chips - 1
        for lane in range(lanes):
            for way in range(2):
                if lane == 0:
                    owns[way, step].wait()
                    pairs[way, step].wait_recv()
                if step > 0:
                    rings[step - 1, way, lane].wait_recv()

                def add(index, carry, way=way, lane=lane):
                    here = pl.ds(pl.multiple_of(index * part, part), part)
                    total = mine[way, step, lane, here, :].astype(jnp.float32)
                    total += pair[way, step, lane, here, :].astype(jnp.float32)
                    if step > 0:
                        total += got[way, step - 1, lane, here, :].astype(jnp.float32)
                    if last:
                        out_ref[way, lane, here, :] = total.astype(out_ref.dtype)
                    else:
                        mine[way, step, lane, here, :] = total.astype(mine.dtype)
                    return carry

                lax.fori_loop(0, high // part, add, 0)
                if not last:
                    copy = send(
                        mine.at[way, step, lane],
                        got.at[way, step, lane],
                        ring_send.at[step, way, lane],
                        ring_recv.at[step, way, lane],
                        nexts[way],
                    )
                    copy.start()
                    rings[step, way, lane] = copy
    for copy in pairs.values():
        copy.wait_send()
    for copy in rings.values():
        copy.wait_send()


def ring_sum(x, chips, collective_id, out_dtype):
    rows, width = x.shape
    rows = rows // (2 * chips)
    lanes = 2 if rows % 64 == 0 else 1
    high = rows // (2 * lanes)
    block = (lanes, high, width)
    out = pl.pallas_call(
        functools.partial(sum_kernel, chips, lanes),
        out_shape=jax.ShapeDtypeStruct((2,) + block, out_dtype),
        in_specs=[pl.BlockSpec(memory_space=pl.ANY)],
        out_specs=pl.BlockSpec(memory_space=pltpu.VMEM),
        scratch_shapes=[
            pltpu.VMEM((2, chips) + block, x.dtype),
            pltpu.VMEM((2, chips) + block, x.dtype),
            pltpu.VMEM((2, chips) + block, x.dtype),
            pltpu.SemaphoreType.DMA((2, chips)),
            pltpu.SemaphoreType.DMA((2, chips)),
            pltpu.SemaphoreType.DMA((2, chips)),
            pltpu.SemaphoreType.DMA((chips, 2, lanes)),
            pltpu.SemaphoreType.DMA((chips, 2, lanes)),
        ],
        compiler_params=pltpu.CompilerParams(
            collective_id=collective_id, has_side_effects=True, vmem_limit_bytes=48 * MIB
        ),
    )(x.reshape((chips, 2, 2) + block))
    return out.reshape(rows, width)


def attend_kernel(group, retrieved, ids_ref, q_ref, g_ref, own_ref, *refs):
    passages = refs[:retrieved]
    dq_ref, dense_ref, down_ref, keys, values, dkeys, dvalues = refs[retrieved:]
    scaling = HD ** (-0.5)
    remote = retrieved * PLEN
    tokens = q_ref.shape[0]
    query = pl.program_id(1)

    @pl.when(query == 0)
    def _():
        def clear(p, carry):
            dense_ref[p] = jnp.zeros(dense_ref.shape[1:], dense_ref.dtype)
            return carry

        lax.fori_loop(0, dense_ref.shape[0], clear, 0)

    for i in range(retrieved):
        keys[i * PLEN : (i + 1) * PLEN, :] = passages[i][0, :, :HD]
        values[i * PLEN : (i + 1) * PLEN, :] = passages[i][0, :, HD:]
    keys[remote:, :] = own_ref[:, :HD]
    values[remote:, :] = own_ref[:, HD:]
    row = lax.broadcasted_iota(jnp.int32, (2 * tokens, tokens), 0)
    col = lax.broadcasted_iota(jnp.int32, (2 * tokens, tokens), 1)
    hidden = col > jnp.where(row >= tokens, row - tokens, row)

    def dot(a, b, dims):
        return lax.dot_general(a, b, ((dims[0], dims[1]), ((), ())), preferred_element_type=jnp.float32)

    for pair in range(group // 2):
        lo, mid, hi = 2 * pair * HD, (2 * pair + 1) * HD, (2 * pair + 2) * HD
        q = jnp.concatenate([q_ref[:, lo:mid], q_ref[:, mid:hi]], axis=0)
        g = jnp.concatenate([g_ref[:, lo:mid], g_ref[:, mid:hi]], axis=0)
        k, v = keys[...], values[...]
        scores = dot(q, k, ((1,), (1,)))
        tail = jnp.where(hidden, jnp.float32(-1e30), scores[:, remote:])
        scores = jnp.concatenate([scores[:, :remote], tail], axis=1)
        largest = jnp.max(scores, axis=1, keepdims=True)
        exponent = jnp.exp2((scores - largest) * jnp.float32(scaling * math.log2(math.e)))
        weights = exponent * (1.0 / jnp.sum(exponent, axis=1, keepdims=True))
        low = weights.astype(jnp.bfloat16)
        outputs = dot(low, v, ((1,), (0,)))
        delta = jnp.sum(outputs * g.astype(jnp.float32), axis=1, keepdims=True)
        grad = (weights * (dot(g, v, ((1,), (1,))) - delta)).astype(jnp.bfloat16)
        dq = (dot(grad, k, ((1,), (0,))) * scaling).astype(dq_ref.dtype)
        dq_ref[:, lo:mid] = dq[:tokens]
        dq_ref[:, mid:hi] = dq[tokens:]
        dk = dot(grad, q, ((0,), (0,)))
        dv = dot(low, g, ((0,), (0,)))
        if pair == 0:
            dkeys[...] = dk
            dvalues[...] = dv
        else:
            dkeys[...] += dk
            dvalues[...] += dv
    for i in range(retrieved):
        p = ids_ref[query * retrieved + i]
        rows = slice(i * PLEN, (i + 1) * PLEN)
        pair = jnp.concatenate([dkeys[rows, :] * scaling, dvalues[rows, :]], axis=1)
        pair = pair.astype(jnp.bfloat16).astype(jnp.float32)
        dense_ref[p] = (dense_ref[p].astype(jnp.float32) + pair).astype(dense_ref.dtype)
    down_ref[:, :HD] = (dkeys[remote:, :] * scaling).astype(down_ref.dtype)
    down_ref[:, HD:] = dvalues[remote:, :].astype(down_ref.dtype)


def attend(ids, queries, out_grad, query_kv, passage_kv, queries_here, retrieved):
    tokens = queries.shape[0] // queries_here
    width = query_kv.shape[1]
    heads = width // (2 * HD)
    wide = queries.shape[1] // heads
    group = wide // HD
    keys = retrieved * PLEN + tokens

    def passage_spec(i):
        return pl.BlockSpec((1, PLEN, 2 * HD), lambda h, n, ids: (ids[n * retrieved + i], 0, h))

    wide_spec = pl.BlockSpec((tokens, wide), lambda h, n, ids: (n, h))
    own_spec = pl.BlockSpec((tokens, 2 * HD), lambda h, n, ids: (n, h))
    flops = 12 * queries_here * heads * group * tokens * keys * HD
    return pl.pallas_call(
        functools.partial(attend_kernel, group, retrieved),
        grid_spec=pltpu.PrefetchScalarGridSpec(
            num_scalar_prefetch=1,
            grid=(heads, queries_here),
            in_specs=[wide_spec, wide_spec, own_spec] + [passage_spec(i) for i in range(retrieved)],
            out_specs=[
                wide_spec,
                pl.BlockSpec((passage_kv.shape[0], PLEN, 2 * HD), lambda h, n, ids: (0, 0, h)),
                own_spec,
            ],
            scratch_shapes=[
                pltpu.VMEM((keys, HD), jnp.bfloat16),
                pltpu.VMEM((keys, HD), jnp.bfloat16),
                pltpu.VMEM((keys, HD), jnp.float32),
                pltpu.VMEM((keys, HD), jnp.float32),
            ],
        ),
        out_shape=[
            jax.ShapeDtypeStruct(queries.shape, jnp.bfloat16),
            jax.ShapeDtypeStruct(passage_kv.shape, jnp.bfloat16),
            jax.ShapeDtypeStruct(query_kv.shape, jnp.bfloat16),
        ],
        compiler_params=pltpu.CompilerParams(vmem_limit_bytes=56 * MIB),
        cost_estimate=pl.CostEstimate(flops=flops, bytes_accessed=16 * MIB, transcendentals=0),
    )(ids, queries, out_grad, query_kv, *([passage_kv] * retrieved))


def per_device(passage_hidden, kv_weight, queries, query_kv, out_grad, source_device, source_slot):
    owners = lax.axis_size("pas")
    shares = lax.axis_size("tp")
    share = lax.axis_index("tp")
    chips = owners // 2
    rows_local = passage_hidden.shape[0]
    local_width = query_kv.shape[1]
    passages_here = rows_local // PLEN
    queries_here, retrieved = source_device.shape
    projected = project(passage_hidden, kv_weight, chips, shares, 0)
    passage_kv = ring_gather(projected, chips, 1)
    passage_kv = passage_kv.reshape(owners * passages_here, PLEN, local_width)
    ids = (source_device * passages_here + source_slot).reshape(-1)
    grad_queries, dense, own_grads = attend(
        ids, queries, out_grad, query_kv, passage_kv, queries_here, retrieved
    )
    dense = dense.reshape(owners * rows_local, local_width)
    grad_kv = ring_sum(dense, chips, 2, jnp.bfloat16)
    full = jnp.zeros((rows_local, shares * local_width), jnp.bfloat16)
    full = lax.dynamic_update_slice_in_dim(full, grad_kv, share * local_width, axis=1)
    for k in range(1, shares):
        route = [(i, (i + k) % shares) for i in range(shares)]
        block = lax.ppermute(grad_kv, "tp", route)
        origin = lax.rem(share + shares - k, shares)
        full = lax.dynamic_update_slice_in_dim(full, block, origin * local_width, axis=1)
    partial = jnp.einsum("rc,rd->cd", full, passage_hidden, preferred_element_type=jnp.float32)
    weight_grad = ring_sum(partial.astype(jnp.bfloat16), chips, 3, jnp.float32)
    return grad_queries, own_grads, weight_grad


def solution(mesh):
    in_specs = (
        P("pas", "tp"),
        P("pas", "tp"),
        P("pas", "tp"),
        P("pas", "tp"),
        P("pas", "tp"),
        P("pas", None),
        P("pas", None),
    )
    out_specs = (P("pas", "tp"), P("pas", "tp"), P("pas", "tp"))
    return jax.shard_map(
        per_device, mesh=mesh, in_specs=in_specs, out_specs=out_specs, check_vma=False
    )
```

```python
import functools
import math
import jax
import jax.numpy as jnp
from jax import lax
from jax.experimental import pallas as pl
from jax.experimental.pallas import tpu as pltpu
from jax.sharding import PartitionSpec as P

HD = 128
PLEN = 128
MIB = 1 << 20


def ring_place(chips):
    me = lax.axis_index("pas")
    core = lax.rem(me, 2)
    chip = lax.div(me, 2)
    side = lax.rem(chip, 2)
    deep = lax.div(chip, 2)
    place = deep + side * (chips - 1 - 2 * deep)

    def chip_at(position):
        q = lax.rem(position + 2 * chips, chips)
        half = lax.div(q, chips // 2)
        return 2 * q + half * (2 * chips - 1 - 4 * q)

    return core, place, chip_at


def greet(others, shares=()):
    barrier = pltpu.get_barrier_semaphore()
    for place in [{"pas": other} for other in others] + [{"tp": other} for other in shares]:
        pl.semaphore_signal(barrier, inc=1, device_id=place, device_id_type=pl.DeviceIdType.MESH)
    pl.semaphore_wait(barrier, len(others) + len(shares))


def send(src, dst, send_sem, recv_sem, other, axis="pas"):
    return pltpu.make_async_remote_copy(
        src_ref=src,
        dst_ref=dst,
        send_sem=send_sem,
        recv_sem=recv_sem,
        device_id={axis: other},
        device_id_type=pl.DeviceIdType.MESH,
    )


def gather_kernel(chips, lanes, x_ref, out_ref, own_sem, ring_send, ring_recv, pair_send, pair_recv):
    core, place, chip_at = ring_place(chips)
    mine = chip_at(place)
    partner = 2 * mine + 1 - core
    nexts = (2 * chip_at(place + 1) + core, 2 * chip_at(place - 1) + core)
    greet((nexts[0], nexts[1], partner))
    rings, pairs = {}, []
    for step in range(chips):
        for lane in range(lanes):
            for way in range(2):
                back = step if way == 0 else -step
                where = chip_at(place - back)
                slot = out_ref.at[where, core, way, lane]
                if step == 0:
                    src = x_ref.at[way, lane]
                else:
                    rings[step - 1, way, lane].wait_recv()
                    src = slot
                if step < chips - 1:
                    copy = send(
                        src, slot, ring_send.at[step, way, lane], ring_recv.at[step, way, lane], nexts[way]
                    )
                    copy.start()
                    rings[step, way, lane] = copy
                copy = send(
                    src, slot, pair_send.at[step, way, lane], pair_recv.at[step, way, lane], partner
                )
                copy.start()
                pairs.append(copy)
        if step == 0:
            own = pltpu.make_async_copy(x_ref, out_ref.at[mine, core], own_sem)
            own.start()
    own.wait()
    for copy in rings.values():
        copy.wait_send()
    for copy in pairs:
        copy.wait()


def ring_gather(x, chips, collective_id):
    rows, width = x.shape
    lanes = 2 if rows % 64 == 0 else 1
    high = rows // (2 * lanes)
    out = pl.pallas_call(
        functools.partial(gather_kernel, chips, lanes),
        out_shape=jax.ShapeDtypeStruct((chips, 2, 2, lanes, high, width), x.dtype),
        in_specs=[pl.BlockSpec(memory_space=pl.ANY)],
        out_specs=pl.BlockSpec(memory_space=pl.ANY),
        scratch_shapes=[
            pltpu.SemaphoreType.DMA,
            pltpu.SemaphoreType.DMA((chips, 2, lanes)),
            pltpu.SemaphoreType.DMA((chips, 2, lanes)),
            pltpu.SemaphoreType.DMA((chips, 2, lanes)),
            pltpu.SemaphoreType.DMA((chips, 2, lanes)),
        ],
        compiler_params=pltpu.CompilerParams(collective_id=collective_id, has_side_effects=True),
    )(x.reshape(2, lanes, high, width))
    return out.reshape(chips * 2 * rows, width)


def project_kernel(
    chips, shares, lanes, hidden_ref, x_ref, out_ref, hidden, weight, joined, part, got,
    own_sem, hidden_sem, ring_send, ring_recv, pair_send, pair_recv, share_send, share_recv,
):
    core, place, chip_at = ring_place(chips)
    share = lax.axis_index("tp")
    mine = chip_at(place)
    partner = 2 * mine + 1 - core
    nexts = (2 * chip_at(place + 1) + core, 2 * chip_at(place - 1) + core)
    load = pltpu.make_async_copy(hidden_ref, hidden, hidden_sem)
    load.start()
    own = pltpu.make_async_copy(x_ref, weight.at[mine, core], own_sem)
    own.start()
    greet(
        (nexts[0], nexts[1], partner),
        [lax.rem(share + k, shares) for k in range(1, shares)],
    )
    rows = hidden.shape[0]
    tile = min(256, rows)
    half = part.shape[2]
    each = half // 2
    group = chips // shares
    rings, pairs = {}, {}

    def chip_of(step, way):
        return chip_at(place - step if way == 0 else place + step)

    def goal(step, way):
        return lax.div(chip_of(step, way), group)

    def share_copy(step, way):
        target = goal(step, way)
        slot = lax.rem(target - share + 2 * shares - 1, shares)
        slot = lax.rem(slot, shares - 1)
        return send(
            part.at[way, step],
            got.at[slot, way, step],
            share_send.at[way, step],
            share_recv.at[slot, way, step],
            target,
            "tp",
        )

    def multiply(step):
        for way in range(2):
            for lane in range(lanes):
                pairs[step, way, lane].wait_recv()
            piece = weight[chip_of(step, way), :, way]
            joined[way * half : (way + 1) * half, :] = piece.reshape(half, piece.shape[-1])

        def one(index, carry):
            here = pl.ds(pl.multiple_of(index * tile, tile), tile)
            product = lax.dot_general(
                joined[...], hidden[here, :], (((1,), (1,)), ((), ())),
                preferred_element_type=jnp.float32,
            )
            part[0, step, :, here] = product[:half]
            part[1, step, :, here] = product[half:]
            return carry

        lax.fori_loop(0, rows // tile, one, 0)
        for way in range(2):

            @pl.when(goal(step, way) != share)
            def _(way=way):
                share_copy(step, way).start()

    for step in range(chips):
        for lane in range(lanes):
            for way in range(2):
                slot = weight.at[chip_of(step, way), core, way, lane]
                if step == 0:
                    src = x_ref.at[way, lane]
                else:
                    rings[step - 1, way, lane].wait_recv()
                    src = slot
                if step < chips - 1:
                    copy = send(
                        src, slot, ring_send.at[step, way, lane], ring_recv.at[step, way, lane], nexts[way]
                    )
                    copy.start()
                    rings[step, way, lane] = copy
                copy = send(
                    src, slot, pair_send.at[step, way, lane], pair_recv.at[step, way, lane], partner
                )
                copy.start()
                pairs[step, way, lane] = copy
        if step == 0:
            load.wait()
            own.wait()
        else:
            multiply(step - 1)
    multiply(chips - 1)
    for step in range(chips):
        for way in range(2):

            @pl.when(goal(step, way) == share)
            def _(step=step, way=way):
                total = part[way, step]
                for slot in range(shares - 1):
                    send(
                        part.at[way, step],
                        got.at[slot, way, step],
                        share_send.at[way, step],
                        share_recv.at[slot, way, step],
                        lax.rem(share + 1, shares),
                        "tp",
                    ).wait_recv()
                    total = total + got[slot, way, step]
                total = total.astype(out_ref.dtype)
                where = lax.rem(chip_of(step, way), group)
                out_ref[where, 0, way] = total[:each]
                out_ref[where, 1, way] = total[each:]

            @pl.when(goal(step, way) != share)
            def _(step=step, way=way):
                share_copy(step, way).wait_send()

    for copy in rings.values():
        copy.wait_send()
    for copy in pairs.values():
        copy.wait_send()


def project(hidden, kv_weight, chips, shares, collective_id):
    rows, width = hidden.shape
    high = kv_weight.shape[0]
    lanes = 2 if high % 64 == 0 else 1
    high = high // (2 * lanes)
    half = 2 * lanes * high
    group = chips // shares
    step_sems = pltpu.SemaphoreType.DMA((chips, 2, lanes))
    out = pl.pallas_call(
        functools.partial(project_kernel, chips, shares, lanes),
        out_shape=jax.ShapeDtypeStruct((group, 2, 2, lanes * high, rows), jnp.bfloat16),
        in_specs=[pl.BlockSpec(memory_space=pl.ANY)] * 2,
        out_specs=pl.BlockSpec(memory_space=pltpu.VMEM),
        scratch_shapes=[
            pltpu.VMEM((rows, width), hidden.dtype),
            pltpu.VMEM((chips, 2, 2, lanes, high, width), kv_weight.dtype),
            pltpu.VMEM((2 * half, width), kv_weight.dtype),
            pltpu.VMEM((2, chips, half, rows), jnp.float32),
            pltpu.VMEM((shares - 1, 2, chips, half, rows), jnp.float32),
            pltpu.SemaphoreType.DMA,
            pltpu.SemaphoreType.DMA,
            step_sems,
            step_sems,
            step_sems,
            step_sems,
            pltpu.SemaphoreType.DMA((2, chips)),
            pltpu.SemaphoreType.DMA((shares - 1, 2, chips)),
        ],
        compiler_params=pltpu.CompilerParams(
            collective_id=collective_id, has_side_effects=True, vmem_limit_bytes=56 * MIB
        ),
    )(hidden, kv_weight.reshape(2, lanes, high, width))
    return out.reshape(group * 2 * 2 * lanes * high, rows).T


def return_kernel(
    chips, shares, lanes, thin, x_ref, hidden_ref, out_ref,
    mine, pair, got, full, hidden, joined, ours, theirs, pair_low, got_low,
    hidden_sem, own_sem, pair_send, pair_recv, ring_send, ring_recv, share_send, share_recv,
    low_pair_send, low_pair_recv, low_ring_send, low_ring_recv,
):
    core, place, chip_at = ring_place(chips)
    share = lax.axis_index("tp")
    partner = 2 * chip_at(place) + 1 - core
    nexts = (2 * chip_at(place + 1) + core, 2 * chip_at(place - 1) + core)
    heads, _, _, _, high, wide = mine.shape
    rows, width = hidden.shape
    local = heads * wide
    load = pltpu.make_async_copy(hidden_ref, hidden, hidden_sem)
    owns, pairs, rings, sent = {}, {}, {}, []
    greet(
        (nexts[0], nexts[1], partner),
        [lax.rem(share + k, shares) for k in range(1, shares)],
    )

    def chip_of(step, way):
        return chip_at(place - 1 - step if way == 0 else place + 1 + step)

    for head in range(heads):
        columns = pl.ds(head * wide, wide)
        for step in range(chips):
            for way in range(2):
                where = chip_of(step, way)
                copy = send(
                    x_ref.at[where, 1 - core, way, :, :, columns],
                    pair.at[head, way, step],
                    pair_send.at[head, way, step],
                    pair_recv.at[head, way, step],
                    partner,
                )
                copy.start()
                pairs[head, way, step] = copy
                sent.append(copy)
                copy = pltpu.make_async_copy(
                    x_ref.at[where, core, way, :, :, columns],
                    mine.at[head, way, step],
                    own_sem.at[head, way, step],
                )
                copy.start()
                owns[head, way, step] = copy
    load.start()

    def share_copy(head, origin, k):
        slot = full.at[pl.ds(pl.multiple_of(origin * local + head * wide, wide), wide)]
        return send(
            slot, slot, share_send.at[head, k - 1], share_recv.at[head, k - 1],
            lax.rem(share + k, shares), "tp",
        )

    def work(head, step):
        last = step == chips - 1
        for lane in range(lanes):
            for way in range(2):
                if lane == 0:
                    owns[head, way, step].wait()
                    pairs[head, way, step].wait_recv()
                if step > 0:
                    rings[head, step - 1, way, lane].wait_recv()
                if last:
                    total = mine[head, way, step, lane].astype(jnp.float32)
                    total += pair[head, way, step, lane].astype(jnp.float32)
                    total += got[head, way, step - 1, lane].astype(jnp.float32)
                    start = pl.multiple_of(share * local + head * wide, wide)
                    there = (way * lanes + lane) * high
                    full[pl.ds(start, wide), there : there + high] = total.T.astype(full.dtype)
                    continue

                def add(index, carry, way=way, lane=lane):
                    here = pl.ds(pl.multiple_of(index * 32, 32), 32)
                    total = mine[head, way, step, lane, here, :].astype(jnp.float32)
                    total += pair[head, way, step, lane, here, :].astype(jnp.float32)
                    if step > 0:
                        total += got[head, way, step - 1, lane, here, :].astype(jnp.float32)
                    mine[head, way, step, lane, here, :] = total.astype(mine.dtype)
                    return carry

                lax.fori_loop(0, high // 32, add, 0)
                copy = send(
                    mine.at[head, way, step, lane],
                    got.at[head, way, step, lane],
                    ring_send.at[head, step, way, lane],
                    ring_recv.at[head, step, way, lane],
                    nexts[way],
                )
                copy.start()
                rings[head, step, way, lane] = copy
                sent.append(copy)
        if last:
            for k in range(1, shares):
                copy = share_copy(head, share, k)
                copy.start()
                sent.append(copy)

    for head in range(heads):
        for step in range(chips):
            if step == chips - 1 and head + 1 < heads:
                work(head + 1, 0)
            if step == 0 and head > 0:
                continue
            work(head, step)
    load.wait()
    for head in range(heads):
        for k in range(1, shares):
            share_copy(head, lax.rem(share + shares - k, shares), k).wait_recv()

    each = joined.shape[0] // 4
    short = each // thin
    tile = min(512, width)
    low_pairs, low_rings = {}, {}

    def multiply(step):
        for way in range(2):
            for other in range(2):
                side = core if other == 0 else 1 - core
                start = ((2 * chip_of(step, way) + side) * 2 + way) * each
                there = (2 * way + other) * each
                joined[there : there + each, :] = full[pl.ds(pl.multiple_of(start, each), each), :]

        def one(index, carry):
            here = pl.ds(pl.multiple_of(index * tile, tile), tile)
            product = jnp.dot(
                joined[...], hidden[:, here], preferred_element_type=jnp.float32
            ).astype(ours.dtype)
            for way in range(2):
                there = 2 * way * each
                ours[way, step, :, here] = product[there : there + each]
                theirs[way, step, :, here] = product[there + each : there + 2 * each]
            return carry

        lax.fori_loop(0, width // tile, one, 0)
        for way in range(2):
            copy = send(
                theirs.at[way, step],
                pair_low.at[way, step],
                low_pair_send.at[way, step],
                low_pair_recv.at[way, step],
                partner,
            )
            copy.start()
            low_pairs[way, step] = copy
            sent.append(copy)

    def pass_on(step):
        last = step == chips - 1
        for lane in range(thin):
            for way in range(2):
                if lane == 0:
                    low_pairs[way, step].wait_recv()
                if step > 0:
                    low_rings[step - 1, way, lane].wait_recv()
                here = slice(lane * short, (lane + 1) * short)

                def add(index, carry, way=way, here=here):
                    there = pl.ds(pl.multiple_of(index * tile, tile), tile)
                    total = ours[way, step, here, there].astype(jnp.float32)
                    total += pair_low[way, step, here, there].astype(jnp.float32)
                    if step > 0:
                        total += got_low[way, step - 1, here, there].astype(jnp.float32)
                    if last:
                        out_ref[way, here, there] = total
                    else:
                        ours[way, step, here, there] = total.astype(ours.dtype)
                    return carry

                lax.fori_loop(0, width // tile, add, 0)
                if not last:
                    copy = send(
                        ours.at[way, step, here],
                        got_low.at[way, step, here],
                        low_ring_send.at[step, way, lane],
                        low_ring_recv.at[step, way, lane],
                        nexts[way],
                    )
                    copy.start()
                    low_rings[step, way, lane] = copy
                    sent.append(copy)

    multiply(0)
    for step in range(chips):
        if step + 1 < chips:
            multiply(step + 1)
        pass_on(step)
    for copy in sent:
        copy.wait_send()


def return_grads(dense, hidden, chips, shares, out_rows, collective_id):
    rows, width = hidden.shape
    local = dense.shape[1]
    wide = 2 * HD
    heads = local // wide
    lanes = 2
    high = rows // (2 * lanes)
    each = out_rows // 2
    thin = 2 if each % 32 == 0 else 1
    slots = pltpu.VMEM((heads, 2, chips, lanes, high, wide), dense.dtype)
    low_slots = pltpu.VMEM((2, chips, each, width), dense.dtype)
    head_sems = pltpu.SemaphoreType.DMA((heads, 2, chips))
    lane_sems = pltpu.SemaphoreType.DMA((heads, chips, 2, lanes))
    share_sems = pltpu.SemaphoreType.DMA((heads, shares - 1))
    low_sems = pltpu.SemaphoreType.DMA((2, chips))
    thin_sems = pltpu.SemaphoreType.DMA((chips, 2, thin))
    out = pl.pallas_call(
        functools.partial(return_kernel, chips, shares, lanes, thin),
        out_shape=jax.ShapeDtypeStruct((2, each, width), jnp.float32),
        in_specs=[pl.BlockSpec(memory_space=pl.ANY)] * 2,
        out_specs=pl.BlockSpec(memory_space=pltpu.VMEM),
        scratch_shapes=[
            slots, slots, slots,
            pltpu.VMEM((shares * local, rows), dense.dtype),
            pltpu.VMEM((rows, width), hidden.dtype),
            pltpu.VMEM((4 * each, rows), dense.dtype),
            low_slots, low_slots, low_slots, low_slots,
            pltpu.SemaphoreType.DMA,
            head_sems, head_sems, head_sems,
            lane_sems, lane_sems,
            share_sems, share_sems,
            low_sems, low_sems,
            thin_sems, thin_sems,
        ],
        compiler_params=pltpu.CompilerParams(
            collective_id=collective_id, has_side_effects=True, vmem_limit_bytes=60 * MIB
        ),
    )(dense.reshape(chips, 2, 2, lanes, high, local), hidden)
    return out.reshape(out_rows, width)


def attend_kernel(group, retrieved, ids_ref, q_ref, g_ref, own_ref, *refs):
    passages = refs[:retrieved]
    dq_ref, dense_ref, down_ref, keys, values, dkeys, dvalues = refs[retrieved:]
    scaling = HD ** (-0.5)
    remote = retrieved * PLEN
    tokens = q_ref.shape[0]
    query = pl.program_id(1)

    @pl.when(query == 0)
    def _():
        def clear(p, carry):
            dense_ref[p] = jnp.zeros(dense_ref.shape[1:], dense_ref.dtype)
            return carry

        lax.fori_loop(0, dense_ref.shape[0], clear, 0)

    for i in range(retrieved):
        keys[i * PLEN : (i + 1) * PLEN, :] = passages[i][0, :, :HD]
        values[i * PLEN : (i + 1) * PLEN, :] = passages[i][0, :, HD:]
    keys[remote:, :] = own_ref[:, :HD]
    values[remote:, :] = own_ref[:, HD:]
    row = lax.broadcasted_iota(jnp.int32, (2 * tokens, tokens), 0)
    col = lax.broadcasted_iota(jnp.int32, (2 * tokens, tokens), 1)
    hidden = col > jnp.where(row >= tokens, row - tokens, row)

    def dot(a, b, dims):
        return lax.dot_general(a, b, ((dims[0], dims[1]), ((), ())), preferred_element_type=jnp.float32)

    for pair in range(group // 2):
        lo, mid, hi = 2 * pair * HD, (2 * pair + 1) * HD, (2 * pair + 2) * HD
        q = jnp.concatenate([q_ref[:, lo:mid], q_ref[:, mid:hi]], axis=0)
        g = jnp.concatenate([g_ref[:, lo:mid], g_ref[:, mid:hi]], axis=0)
        k, v = keys[...], values[...]
        scores = dot(q, k, ((1,), (1,)))
        tail = jnp.where(hidden, jnp.float32(-1e30), scores[:, remote:])
        scores = jnp.concatenate([scores[:, :remote], tail], axis=1)
        largest = jnp.max(scores, axis=1, keepdims=True)
        exponent = jnp.exp2((scores - largest) * jnp.float32(scaling * math.log2(math.e)))
        weights = exponent * (1.0 / jnp.sum(exponent, axis=1, keepdims=True))
        low = weights.astype(jnp.bfloat16)
        outputs = dot(low, v, ((1,), (0,)))
        delta = jnp.sum(outputs * g.astype(jnp.float32), axis=1, keepdims=True)
        grad = (weights * (dot(g, v, ((1,), (1,))) - delta)).astype(jnp.bfloat16)
        dq = (dot(grad, k, ((1,), (0,))) * scaling).astype(dq_ref.dtype)
        dq_ref[:, lo:mid] = dq[:tokens]
        dq_ref[:, mid:hi] = dq[tokens:]
        dk = dot(grad, q, ((0,), (0,)))
        dv = dot(low, g, ((0,), (0,)))
        if pair == 0:
            dkeys[...] = dk
            dvalues[...] = dv
        else:
            dkeys[...] += dk
            dvalues[...] += dv
    for i in range(retrieved):
        p = ids_ref[query * retrieved + i]
        rows = slice(i * PLEN, (i + 1) * PLEN)
        pair = jnp.concatenate([dkeys[rows, :] * scaling, dvalues[rows, :]], axis=1)
        pair = pair.astype(jnp.bfloat16).astype(jnp.float32)
        dense_ref[p] = (dense_ref[p].astype(jnp.float32) + pair).astype(dense_ref.dtype)
    down_ref[:, :HD] = (dkeys[remote:, :] * scaling).astype(down_ref.dtype)
    down_ref[:, HD:] = dvalues[remote:, :].astype(down_ref.dtype)


def attend(ids, queries, out_grad, query_kv, passage_kv, queries_here, retrieved):
    tokens = queries.shape[0] // queries_here
    width = query_kv.shape[1]
    heads = width // (2 * HD)
    wide = queries.shape[1] // heads
    group = wide // HD
    keys = retrieved * PLEN + tokens

    def passage_spec(i):
        return pl.BlockSpec((1, PLEN, 2 * HD), lambda h, n, ids: (ids[n * retrieved + i], 0, h))

    wide_spec = pl.BlockSpec((tokens, wide), lambda h, n, ids: (n, h))
    own_spec = pl.BlockSpec((tokens, 2 * HD), lambda h, n, ids: (n, h))
    flops = 12 * queries_here * heads * group * tokens * keys * HD
    return pl.pallas_call(
        functools.partial(attend_kernel, group, retrieved),
        grid_spec=pltpu.PrefetchScalarGridSpec(
            num_scalar_prefetch=1,
            grid=(heads, queries_here),
            in_specs=[wide_spec, wide_spec, own_spec] + [passage_spec(i) for i in range(retrieved)],
            out_specs=[
                wide_spec,
                pl.BlockSpec((passage_kv.shape[0], PLEN, 2 * HD), lambda h, n, ids: (0, 0, h)),
                own_spec,
            ],
            scratch_shapes=[
                pltpu.VMEM((keys, HD), jnp.bfloat16),
                pltpu.VMEM((keys, HD), jnp.bfloat16),
                pltpu.VMEM((keys, HD), jnp.float32),
                pltpu.VMEM((keys, HD), jnp.float32),
            ],
        ),
        out_shape=[
            jax.ShapeDtypeStruct(queries.shape, jnp.bfloat16),
            jax.ShapeDtypeStruct(passage_kv.shape, jnp.bfloat16),
            jax.ShapeDtypeStruct(query_kv.shape, jnp.bfloat16),
        ],
        compiler_params=pltpu.CompilerParams(vmem_limit_bytes=56 * MIB),
        cost_estimate=pl.CostEstimate(flops=flops, bytes_accessed=16 * MIB, transcendentals=0),
    )(ids, queries, out_grad, query_kv, *([passage_kv] * retrieved))


def per_device(passage_hidden, kv_weight, queries, query_kv, out_grad, source_device, source_slot):
    owners = lax.axis_size("pas")
    shares = lax.axis_size("tp")
    share = lax.axis_index("tp")
    chips = owners // 2
    rows_local = passage_hidden.shape[0]
    local_width = query_kv.shape[1]
    passages_here = rows_local // PLEN
    queries_here, retrieved = source_device.shape
    projected = project(passage_hidden, kv_weight, chips, shares, 0)
    passage_kv = ring_gather(projected, chips, 1)
    passage_kv = passage_kv.reshape(owners * passages_here, PLEN, local_width)
    ids = (source_device * passages_here + source_slot).reshape(-1)
    grad_queries, dense, own_grads = attend(
        ids, queries, out_grad, query_kv, passage_kv, queries_here, retrieved
    )
    dense = dense.reshape(owners * rows_local, local_width)
    weight_grad = return_grads(dense, passage_hidden, chips, shares, kv_weight.shape[0], 2)
    return grad_queries, own_grads, weight_grad


def solution(mesh):
    in_specs = (
        P("pas", "tp"),
        P("pas", "tp"),
        P("pas", "tp"),
        P("pas", "tp"),
        P("pas", "tp"),
        P("pas", None),
        P("pas", None),
    )
    out_specs = (P("pas", "tp"), P("pas", "tp"), P("pas", "tp"))
    return jax.shard_map(
        per_device, mesh=mesh, in_specs=in_specs, out_specs=out_specs, check_vma=False
    )
```

```python
import functools
import math
import jax
import jax.numpy as jnp
from jax import lax
from jax.experimental import pallas as pl
from jax.experimental.pallas import tpu as pltpu
from jax.sharding import PartitionSpec as P

HD = 128
PLEN = 128
MIB = 1 << 20


def ring_place(chips):
    me = lax.axis_index("pas")
    core = lax.rem(me, 2)
    chip = lax.div(me, 2)
    side = lax.rem(chip, 2)
    deep = lax.div(chip, 2)
    place = deep + side * (chips - 1 - 2 * deep)

    def chip_at(position):
        q = lax.rem(position + 2 * chips, chips)
        half = lax.div(q, chips // 2)
        return 2 * q + half * (2 * chips - 1 - 4 * q)

    return core, place, chip_at


def greet(others, shares=()):
    barrier = pltpu.get_barrier_semaphore()
    for place in [{"pas": other} for other in others] + [{"tp": other} for other in shares]:
        pl.semaphore_signal(barrier, inc=1, device_id=place, device_id_type=pl.DeviceIdType.MESH)
    pl.semaphore_wait(barrier, len(others) + len(shares))


def send(src, dst, send_sem, recv_sem, other, axis="pas"):
    return pltpu.make_async_remote_copy(
        src_ref=src,
        dst_ref=dst,
        send_sem=send_sem,
        recv_sem=recv_sem,
        device_id={axis: other},
        device_id_type=pl.DeviceIdType.MESH,
    )


def gather_kernel(chips, lanes, x_ref, out_ref, own_sem, ring_send, ring_recv, pair_send, pair_recv):
    core, place, chip_at = ring_place(chips)
    mine = chip_at(place)
    partner = 2 * mine + 1 - core
    nexts = (2 * chip_at(place + 1) + core, 2 * chip_at(place - 1) + core)
    greet((nexts[0], nexts[1], partner))
    rings, pairs = {}, []
    for step in range(chips):
        for lane in range(lanes):
            for way in range(2):
                back = step if way == 0 else -step
                where = chip_at(place - back)
                slot = out_ref.at[where, core, way, lane]
                if step == 0:
                    src = x_ref.at[way, lane]
                else:
                    rings[step - 1, way, lane].wait_recv()
                    src = slot
                if step < chips - 1:
                    copy = send(
                        src, slot, ring_send.at[step, way, lane], ring_recv.at[step, way, lane], nexts[way]
                    )
                    copy.start()
                    rings[step, way, lane] = copy
                copy = send(
                    src, slot, pair_send.at[step, way, lane], pair_recv.at[step, way, lane], partner
                )
                copy.start()
                pairs.append(copy)
        if step == 0:
            own = pltpu.make_async_copy(x_ref, out_ref.at[mine, core], own_sem)
            own.start()
    own.wait()
    for copy in rings.values():
        copy.wait_send()
    for copy in pairs:
        copy.wait()


def ring_gather(x, chips, collective_id):
    rows, width = x.shape
    lanes = 2 if rows % 64 == 0 else 1
    high = rows // (2 * lanes)
    out = pl.pallas_call(
        functools.partial(gather_kernel, chips, lanes),
        out_shape=jax.ShapeDtypeStruct((chips, 2, 2, lanes, high, width), x.dtype),
        in_specs=[pl.BlockSpec(memory_space=pl.ANY)],
        out_specs=pl.BlockSpec(memory_space=pl.ANY),
        scratch_shapes=[
            pltpu.SemaphoreType.DMA,
            pltpu.SemaphoreType.DMA((chips, 2, lanes)),
            pltpu.SemaphoreType.DMA((chips, 2, lanes)),
            pltpu.SemaphoreType.DMA((chips, 2, lanes)),
            pltpu.SemaphoreType.DMA((chips, 2, lanes)),
        ],
        compiler_params=pltpu.CompilerParams(collective_id=collective_id, has_side_effects=True),
    )(x.reshape(2, lanes, high, width))
    return out.reshape(chips * 2 * rows, width)


def project_kernel(
    chips, shares, lanes, hidden_ref, x_ref, out_ref, hidden, weight, joined, part, got,
    own_sem, hidden_sem, ring_send, ring_recv, pair_send, pair_recv, share_send, share_recv,
):
    core, place, chip_at = ring_place(chips)
    share = lax.axis_index("tp")
    mine = chip_at(place)
    partner = 2 * mine + 1 - core
    nexts = (2 * chip_at(place + 1) + core, 2 * chip_at(place - 1) + core)
    load = pltpu.make_async_copy(hidden_ref, hidden, hidden_sem)
    load.start()
    own = pltpu.make_async_copy(x_ref, weight.at[mine, core], own_sem)
    own.start()
    greet(
        (nexts[0], nexts[1], partner),
        [lax.rem(share + k, shares) for k in range(1, shares)],
    )
    rows = hidden.shape[0]
    tile = min(256, rows)
    half = part.shape[2]
    each = half // 2
    group = chips // shares
    rings, pairs = {}, {}

    def chip_of(step, way):
        return chip_at(place - step if way == 0 else place + step)

    def goal(step, way):
        return lax.div(chip_of(step, way), group)

    def share_copy(step, way):
        target = goal(step, way)
        slot = lax.rem(target - share + 2 * shares - 1, shares)
        slot = lax.rem(slot, shares - 1)
        return send(
            part.at[way, step],
            got.at[slot, way, step],
            share_send.at[way, step],
            share_recv.at[slot, way, step],
            target,
            "tp",
        )

    def multiply(step):
        for way in range(2):
            for lane in range(lanes):
                pairs[step, way, lane].wait_recv()
            piece = weight[chip_of(step, way), :, way]
            joined[way * half : (way + 1) * half, :] = piece.reshape(half, piece.shape[-1])

        def one(index, carry):
            here = pl.ds(pl.multiple_of(index * tile, tile), tile)
            product = lax.dot_general(
                joined[...], hidden[here, :], (((1,), (1,)), ((), ())),
                preferred_element_type=jnp.float32,
            )
            part[0, step, :, here] = product[:half]
            part[1, step, :, here] = product[half:]
            return carry

        lax.fori_loop(0, rows // tile, one, 0)
        for way in range(2):

            @pl.when(goal(step, way) != share)
            def _(way=way):
                share_copy(step, way).start()

    for step in range(chips):
        for lane in range(lanes):
            for way in range(2):
                slot = weight.at[chip_of(step, way), core, way, lane]
                if step == 0:
                    src = x_ref.at[way, lane]
                else:
                    rings[step - 1, way, lane].wait_recv()
                    src = slot
                if step < chips - 1:
                    copy = send(
                        src, slot, ring_send.at[step, way, lane], ring_recv.at[step, way, lane], nexts[way]
                    )
                    copy.start()
                    rings[step, way, lane] = copy
                copy = send(
                    src, slot, pair_send.at[step, way, lane], pair_recv.at[step, way, lane], partner
                )
                copy.start()
                pairs[step, way, lane] = copy
        if step == 0:
            load.wait()
            own.wait()
        else:
            multiply(step - 1)
    multiply(chips - 1)
    for step in range(chips):
        for way in range(2):

            @pl.when(goal(step, way) == share)
            def _(step=step, way=way):
                total = part[way, step]
                for slot in range(shares - 1):
                    send(
                        part.at[way, step],
                        got.at[slot, way, step],
                        share_send.at[way, step],
                        share_recv.at[slot, way, step],
                        lax.rem(share + 1, shares),
                        "tp",
                    ).wait_recv()
                    total = total + got[slot, way, step]
                total = total.astype(out_ref.dtype)
                where = lax.rem(chip_of(step, way), group)
                out_ref[where, 0, way] = total[:each]
                out_ref[where, 1, way] = total[each:]

            @pl.when(goal(step, way) != share)
            def _(step=step, way=way):
                share_copy(step, way).wait_send()

    for copy in rings.values():
        copy.wait_send()
    for copy in pairs.values():
        copy.wait_send()


def project(hidden, kv_weight, chips, shares, collective_id):
    rows, width = hidden.shape
    high = kv_weight.shape[0]
    lanes = 2 if high % 64 == 0 else 1
    high = high // (2 * lanes)
    half = 2 * lanes * high
    group = chips // shares
    step_sems = pltpu.SemaphoreType.DMA((chips, 2, lanes))
    out = pl.pallas_call(
        functools.partial(project_kernel, chips, shares, lanes),
        out_shape=jax.ShapeDtypeStruct((group, 2, 2, lanes * high, rows), jnp.bfloat16),
        in_specs=[pl.BlockSpec(memory_space=pl.ANY)] * 2,
        out_specs=pl.BlockSpec(memory_space=pltpu.VMEM),
        scratch_shapes=[
            pltpu.VMEM((rows, width), hidden.dtype),
            pltpu.VMEM((chips, 2, 2, lanes, high, width), kv_weight.dtype),
            pltpu.VMEM((2 * half, width), kv_weight.dtype),
            pltpu.VMEM((2, chips, half, rows), jnp.float32),
            pltpu.VMEM((shares - 1, 2, chips, half, rows), jnp.float32),
            pltpu.SemaphoreType.DMA,
            pltpu.SemaphoreType.DMA,
            step_sems,
            step_sems,
            step_sems,
            step_sems,
            pltpu.SemaphoreType.DMA((2, chips)),
            pltpu.SemaphoreType.DMA((shares - 1, 2, chips)),
        ],
        compiler_params=pltpu.CompilerParams(
            collective_id=collective_id, has_side_effects=True, vmem_limit_bytes=56 * MIB
        ),
    )(hidden, kv_weight.reshape(2, lanes, high, width))
    return out.reshape(group * 2 * 2 * lanes * high, rows).T


def return_kernel(
    chips, shares, lanes, thin, x_ref, hidden_ref, out_ref,
    mine, pair, got, full, hidden, joined, ours, theirs, pair_low, got_low,
    hidden_sem, own_sem, pair_send, pair_recv, ring_send, ring_recv, share_send, share_recv,
    low_pair_send, low_pair_recv, low_ring_send, low_ring_recv,
):
    core, place, chip_at = ring_place(chips)
    share = lax.axis_index("tp")
    partner = 2 * chip_at(place) + 1 - core
    nexts = (2 * chip_at(place + 1) + core, 2 * chip_at(place - 1) + core)
    heads, _, _, _, high, wide = mine.shape
    rows, width = hidden.shape
    local = heads * wide
    load = pltpu.make_async_copy(hidden_ref, hidden, hidden_sem)
    owns, pairs, rings, sent = {}, {}, {}, []
    greet(
        (nexts[0], nexts[1], partner),
        [lax.rem(share + k, shares) for k in range(1, shares)],
    )

    def chip_of(step, way):
        return chip_at(place - 1 - step if way == 0 else place + 1 + step)

    for head in range(heads):
        columns = pl.ds(head * wide, wide)
        for step in range(chips):
            for way in range(2):
                where = chip_of(step, way)
                copy = send(
                    x_ref.at[where, 1 - core, way, :, :, columns],
                    pair.at[head, way, step],
                    pair_send.at[head, way, step],
                    pair_recv.at[head, way, step],
                    partner,
                )
                copy.start()
                pairs[head, way, step] = copy
                sent.append(copy)
                copy = pltpu.make_async_copy(
                    x_ref.at[where, core, way, :, :, columns],
                    mine.at[head, way, step],
                    own_sem.at[head, way, step],
                )
                copy.start()
                owns[head, way, step] = copy
    load.start()

    def share_copy(head, origin, k):
        slot = full.at[pl.ds(pl.multiple_of(origin * local + head * wide, wide), wide)]
        return send(
            slot, slot, share_send.at[head, k - 1], share_recv.at[head, k - 1],
            lax.rem(share + k, shares), "tp",
        )

    def work(head, step):
        last = step == chips - 1
        for lane in range(lanes):
            for way in range(2):
                if lane == 0:
                    owns[head, way, step].wait()
                    pairs[head, way, step].wait_recv()
                if step > 0:
                    rings[head, step - 1, way, lane].wait_recv()
                if last:
                    total = mine[head, way, step, lane].astype(jnp.float32)
                    total += pair[head, way, step, lane].astype(jnp.float32)
                    total += got[head, way, step - 1, lane].astype(jnp.float32)
                    start = pl.multiple_of(share * local + head * wide, wide)
                    there = (way * lanes + lane) * high
                    full[pl.ds(start, wide), there : there + high] = total.T.astype(full.dtype)
                    continue

                def add(index, carry, way=way, lane=lane):
                    here = pl.ds(pl.multiple_of(index * 32, 32), 32)
                    total = mine[head, way, step, lane, here, :].astype(jnp.float32)
                    total += pair[head, way, step, lane, here, :].astype(jnp.float32)
                    if step > 0:
                        total += got[head, way, step - 1, lane, here, :].astype(jnp.float32)
                    mine[head, way, step, lane, here, :] = total.astype(mine.dtype)
                    return carry

                lax.fori_loop(0, high // 32, add, 0)
                copy = send(
                    mine.at[head, way, step, lane],
                    got.at[head, way, step, lane],
                    ring_send.at[head, step, way, lane],
                    ring_recv.at[head, step, way, lane],
                    nexts[way],
                )
                copy.start()
                rings[head, step, way, lane] = copy
                sent.append(copy)
        if last:
            for k in range(1, shares):
                copy = share_copy(head, share, k)
                copy.start()
                sent.append(copy)

    for head in range(heads):
        for step in range(chips):
            if step == chips - 1 and head + 1 < heads:
                work(head + 1, 0)
            if step == 0 and head > 0:
                continue
            work(head, step)
    load.wait()
    for head in range(heads):
        for k in range(1, shares):
            share_copy(head, lax.rem(share + shares - k, shares), k).wait_recv()

    each = joined.shape[0] // 4
    short = each // thin
    tile = min(512, width)
    low_pairs, low_rings = {}, {}

    def multiply(step):
        for way in range(2):
            for other in range(2):
                side = core if other == 0 else 1 - core
                start = ((2 * chip_of(step, way) + side) * 2 + way) * each
                there = (2 * way + other) * each
                joined[there : there + each, :] = full[pl.ds(pl.multiple_of(start, each), each), :]

        def one(index, carry):
            here = pl.ds(pl.multiple_of(index * tile, tile), tile)
            product = jnp.dot(
                joined[...], hidden[:, here], preferred_element_type=jnp.float32
            ).astype(ours.dtype)
            for way in range(2):
                there = 2 * way * each
                ours[way, step, :, here] = product[there : there + each]
                theirs[way, step, :, here] = product[there + each : there + 2 * each]
            return carry

        lax.fori_loop(0, width // tile, one, 0)
        for way in range(2):
            copy = send(
                theirs.at[way, step],
                pair_low.at[way, step],
                low_pair_send.at[way, step],
                low_pair_recv.at[way, step],
                partner,
            )
            copy.start()
            low_pairs[way, step] = copy
            sent.append(copy)

    def pass_on(step):
        last = step == chips - 1
        for lane in range(thin):
            for way in range(2):
                if lane == 0:
                    low_pairs[way, step].wait_recv()
                if step > 0:
                    low_rings[step - 1, way, lane].wait_recv()
                here = slice(lane * short, (lane + 1) * short)

                def add(index, carry, way=way, here=here):
                    there = pl.ds(pl.multiple_of(index * tile, tile), tile)
                    total = ours[way, step, here, there].astype(jnp.float32)
                    total += pair_low[way, step, here, there].astype(jnp.float32)
                    if step > 0:
                        total += got_low[way, step - 1, here, there].astype(jnp.float32)
                    if last:
                        out_ref[way, here, there] = total
                    else:
                        ours[way, step, here, there] = total.astype(ours.dtype)
                    return carry

                lax.fori_loop(0, width // tile, add, 0)
                if not last:
                    copy = send(
                        ours.at[way, step, here],
                        got_low.at[way, step, here],
                        low_ring_send.at[step, way, lane],
                        low_ring_recv.at[step, way, lane],
                        nexts[way],
                    )
                    copy.start()
                    low_rings[step, way, lane] = copy
                    sent.append(copy)

    multiply(0)
    for step in range(chips):
        if step + 1 < chips:
            multiply(step + 1)
        pass_on(step)
    for copy in sent:
        copy.wait_send()


def return_grads(dense, hidden, chips, shares, out_rows, collective_id):
    rows, width = hidden.shape
    local = dense.shape[1]
    wide = 2 * HD
    heads = local // wide
    lanes = 2
    high = rows // (2 * lanes)
    each = out_rows // 2
    thin = 2 if each % 32 == 0 else 1
    slots = pltpu.VMEM((heads, 2, chips, lanes, high, wide), dense.dtype)
    low_slots = pltpu.VMEM((2, chips, each, width), dense.dtype)
    head_sems = pltpu.SemaphoreType.DMA((heads, 2, chips))
    lane_sems = pltpu.SemaphoreType.DMA((heads, chips, 2, lanes))
    share_sems = pltpu.SemaphoreType.DMA((heads, shares - 1))
    low_sems = pltpu.SemaphoreType.DMA((2, chips))
    thin_sems = pltpu.SemaphoreType.DMA((chips, 2, thin))
    out = pl.pallas_call(
        functools.partial(return_kernel, chips, shares, lanes, thin),
        out_shape=jax.ShapeDtypeStruct((2, each, width), jnp.float32),
        in_specs=[pl.BlockSpec(memory_space=pl.ANY)] * 2,
        out_specs=pl.BlockSpec(memory_space=pltpu.VMEM),
        scratch_shapes=[
            slots, slots, slots,
            pltpu.VMEM((shares * local, rows), dense.dtype),
            pltpu.VMEM((rows, width), hidden.dtype),
            pltpu.VMEM((4 * each, rows), dense.dtype),
            low_slots, low_slots, low_slots, low_slots,
            pltpu.SemaphoreType.DMA,
            head_sems, head_sems, head_sems,
            lane_sems, lane_sems,
            share_sems, share_sems,
            low_sems, low_sems,
            thin_sems, thin_sems,
        ],
        compiler_params=pltpu.CompilerParams(
            collective_id=collective_id, has_side_effects=True, vmem_limit_bytes=60 * MIB
        ),
    )(dense.reshape(chips, 2, 2, lanes, high, local), hidden)
    return out.reshape(out_rows, width)


def attend_rows(
    group, retrieved, rows, passage, q_ref, g_ref, own_ref, dq_ref, keys, values, dkeys, dvalues, between
):
    scaling = HD ** (-0.5)
    remote = retrieved * PLEN
    tokens = keys.shape[0] - remote
    for i in range(retrieved):
        block = passage(i)
        keys[i * PLEN : (i + 1) * PLEN, :] = block[:, :HD]
        values[i * PLEN : (i + 1) * PLEN, :] = block[:, HD:]
    keys[remote:, :] = own_ref[rows, :HD]
    values[remote:, :] = own_ref[rows, HD:]
    row = lax.broadcasted_iota(jnp.int32, (2 * tokens, tokens), 0)
    col = lax.broadcasted_iota(jnp.int32, (2 * tokens, tokens), 1)
    hidden = col > jnp.where(row >= tokens, row - tokens, row)

    def dot(a, b, dims):
        return lax.dot_general(a, b, ((dims[0], dims[1]), ((), ())), preferred_element_type=jnp.float32)

    for pair in range(group // 2):
        lo, mid, hi = 2 * pair * HD, (2 * pair + 1) * HD, (2 * pair + 2) * HD
        q = jnp.concatenate([q_ref[rows, lo:mid], q_ref[rows, mid:hi]], axis=0)
        g = jnp.concatenate([g_ref[rows, lo:mid], g_ref[rows, mid:hi]], axis=0)
        k, v = keys[...], values[...]
        scores = dot(q, k, ((1,), (1,)))
        tail = jnp.where(hidden, jnp.float32(-1e30), scores[:, remote:])
        scores = jnp.concatenate([scores[:, :remote], tail], axis=1)
        largest = jnp.max(scores, axis=1, keepdims=True)
        exponent = jnp.exp2((scores - largest) * jnp.float32(scaling * math.log2(math.e)))
        weights = exponent * (1.0 / jnp.sum(exponent, axis=1, keepdims=True))
        low = weights.astype(jnp.bfloat16)
        outputs = dot(low, v, ((1,), (0,)))
        delta = jnp.sum(outputs * g.astype(jnp.float32), axis=1, keepdims=True)
        grad = (weights * (dot(g, v, ((1,), (1,))) - delta)).astype(jnp.bfloat16)
        dq = (dot(grad, k, ((1,), (0,))) * scaling).astype(dq_ref.dtype)
        dq_ref[rows, lo:mid] = dq[:tokens]
        dq_ref[rows, mid:hi] = dq[tokens:]
        dk = dot(grad, q, ((0,), (0,)))
        dv = dot(low, g, ((0,), (0,)))
        if pair == 0:
            dkeys[...] = dk
            dvalues[...] = dv
        else:
            dkeys[...] += dk
            dvalues[...] += dv
        between(pair)


def grad_rows(rows, dkeys, dvalues):
    scaling = HD ** (-0.5)
    both = jnp.concatenate([dkeys[rows, :] * scaling, dvalues[rows, :]], axis=1)
    return both.astype(jnp.bfloat16)


def early_kernel(
    chips, group, retrieved, ids_ref, x_ref, q_ref, g_ref, own_ref,
    late_ref, dq_ref, remote_ref, down_ref, early, keys, values, dkeys, dvalues,
    own_sem, ring_send, ring_recv, pair_send, pair_recv,
):
    core, place, chip_at = ring_place(chips)
    mine = chip_at(place)
    partner = 2 * mine + 1 - core
    nexts = (2 * chip_at(place + 1) + core, 2 * chip_at(place - 1) + core)
    here = x_ref.shape[0]
    per = here // 4
    wide = 2 * HD
    remote = retrieved * PLEN
    tokens = keys.shape[0] - remote
    targets = (early, late_ref)

    def first(step, way, lane, side):
        where = chip_at(place - step if way == 0 else place + step)
        return (2 * where + side) * here + (2 * way + lane) * per

    def block(head, step, way, lane):
        return targets[head].at[pl.ds(first(step, way, lane, core), per)]

    def source(head, way, lane):
        return x_ref.at[pl.ds((2 * way + lane) * per, per), :, pl.ds(head * wide, wide)]

    def ring_copy(head, step, way, lane, src):
        return send(
            src, block(head, step, way, lane),
            ring_send.at[head, step, way, lane], ring_recv.at[head, step, way, lane], nexts[way],
        )

    def pair_copy(head, step, way, lane, src):
        return send(
            src, block(head, step, way, lane),
            pair_send.at[head, step, way, lane], pair_recv.at[head, step, way, lane], partner,
        )

    def own_copy(head):
        return pltpu.make_async_copy(
            x_ref.at[:, :, pl.ds(head * wide, wide)],
            targets[head].at[pl.ds((2 * mine + core) * here, here)],
            own_sem.at[head],
        )

    def begin(head):
        for lane in range(2):
            for way in range(2):
                ring_copy(head, 0, way, lane, source(head, way, lane)).start()
                pair_copy(head, 0, way, lane, source(head, way, lane)).start()
        own_copy(head).start()

    def serve(head, step):
        for lane in range(2):
            for way in range(2):
                slot = block(head, step, way, lane)
                ring_copy(head, step - 1, way, lane, slot).wait_recv()

                @pl.when(step < chips - 1)
                def _(way=way, lane=lane, slot=slot):
                    ring_copy(head, step, way, lane, slot).start()

                pair_copy(head, step, way, lane, slot).start()

    def finish_pairs(head):
        def one(step, carry):
            for lane in range(2):
                for way in range(2):
                    pair_copy(head, step, way, lane, block(head, step, way, lane)).wait_recv()
            return carry

        lax.fori_loop(0, chips, one, 0)
        own_copy(head).wait()

    greet((nexts[0], nexts[1], partner))
    begin(0)

    def steps(step, carry):
        serve(0, step)
        return carry

    lax.fori_loop(1, chips - 1, steps, 0)
    begin(1)
    serve(0, chips - 1)
    finish_pairs(0)

    def one_query(query, carry):
        rows = pl.ds(pl.multiple_of(query * tokens, tokens), tokens)

        def between(pair):
            if pair % 2 == 1 and pair < 4:
                step = 2 * query + 1 + pair // 2

                @pl.when(step < chips)
                def _():
                    serve(1, step)

        attend_rows(
            group, retrieved, rows, lambda i: early[ids_ref[query * retrieved + i]],
            q_ref, g_ref, own_ref, dq_ref, keys, values, dkeys, dvalues, between,
        )
        for i in range(retrieved):
            remote_ref[query * retrieved + i] = grad_rows(
                slice(i * PLEN, (i + 1) * PLEN), dkeys, dvalues
            )
        down_ref[rows, :] = grad_rows(slice(remote, remote + tokens), dkeys, dvalues)
        return carry

    lax.fori_loop(0, q_ref.shape[0] // tokens, one_query, 0)
    finish_pairs(1)

    def sent(step, carry):
        for head in range(2):
            for lane in range(2):
                for way in range(2):
                    slot = block(head, step, way, lane)
                    pair_copy(head, step, way, lane, slot).wait_send()

                    @pl.when(step < chips - 1)
                    def _(head=head, way=way, lane=lane, slot=slot):
                        ring_copy(head, step, way, lane, slot).wait_send()

        return carry

    lax.fori_loop(0, chips, sent, 0)


def early_attend(ids, queries, out_grad, query_kv, projected, chips, queries_here, retrieved, collective_id):
    rows, _ = projected.shape
    here = rows // PLEN
    total = 2 * chips * here
    wide = 2 * HD
    heads = query_kv.shape[1] // wide
    broad = queries.shape[1] // heads
    tokens = queries.shape[0] // queries_here
    keys = retrieved * PLEN + tokens
    sems = pltpu.SemaphoreType.DMA((2, chips, 2, 2))
    return pl.pallas_call(
        functools.partial(early_kernel, chips, broad // HD, retrieved),
        grid=(1,),
        out_shape=[
            jax.ShapeDtypeStruct((total, PLEN, wide), jnp.bfloat16),
            jax.ShapeDtypeStruct((queries.shape[0], broad), jnp.bfloat16),
            jax.ShapeDtypeStruct((queries_here * retrieved, PLEN, wide), jnp.bfloat16),
            jax.ShapeDtypeStruct((queries.shape[0], wide), jnp.bfloat16),
        ],
        in_specs=[
            pl.BlockSpec(memory_space=pltpu.SMEM),
            pl.BlockSpec(memory_space=pl.ANY),
            pl.BlockSpec((queries.shape[0], broad), lambda i: (0, 0)),
            pl.BlockSpec((queries.shape[0], broad), lambda i: (0, 0)),
            pl.BlockSpec((queries.shape[0], wide), lambda i: (0, 0)),
        ],
        out_specs=[
            pl.BlockSpec(memory_space=pl.ANY),
            pl.BlockSpec((queries.shape[0], broad), lambda i: (0, 0)),
            pl.BlockSpec((queries_here * retrieved, PLEN, wide), lambda i: (0, 0, 0)),
            pl.BlockSpec((queries.shape[0], wide), lambda i: (0, 0)),
        ],
        scratch_shapes=[
            pltpu.VMEM((total, PLEN, wide), jnp.bfloat16),
            pltpu.VMEM((keys, HD), jnp.bfloat16),
            pltpu.VMEM((keys, HD), jnp.bfloat16),
            pltpu.VMEM((keys, HD), jnp.float32),
            pltpu.VMEM((keys, HD), jnp.float32),
            pltpu.SemaphoreType.DMA((2,)),
            sems, sems, sems, sems,
        ],
        compiler_params=pltpu.CompilerParams(
            collective_id=collective_id, has_side_effects=True, vmem_limit_bytes=56 * MIB
        ),
    )(ids, projected.reshape(here, PLEN, -1), queries, out_grad, query_kv)


def attend_kernel(group, retrieved, ready, ids_ref, q_ref, g_ref, own_ref, *refs):
    done, refs = refs[: 3 * ready], refs[3 * ready :]
    passages = refs[:retrieved]
    dq_ref, dense_ref, down_ref, keys, values, dkeys, dvalues = refs[retrieved:]
    remote = retrieved * PLEN
    tokens = q_ref.shape[0]
    head, query = pl.program_id(0), pl.program_id(1)

    @pl.when(query == 0)
    def _():
        def clear(p, carry):
            dense_ref[p] = jnp.zeros(dense_ref.shape[1:], dense_ref.dtype)
            return carry

        lax.fori_loop(0, dense_ref.shape[0], clear, 0)

    def place(i, block):
        p = ids_ref[query * retrieved + i]
        total = dense_ref[p].astype(jnp.float32) + block.astype(jnp.float32)
        dense_ref[p] = total.astype(dense_ref.dtype)

    if ready:

        @pl.when(head == 0)
        def _():
            for i in range(retrieved):
                place(i, done[1][i])
            dq_ref[...] = done[0][...]
            down_ref[...] = done[2][...]

    @pl.when(head >= ready)
    def _():
        attend_rows(
            group, retrieved, slice(0, tokens), lambda i: passages[i][0],
            q_ref, g_ref, own_ref, dq_ref, keys, values, dkeys, dvalues, lambda pair: None,
        )
        for i in range(retrieved):
            place(i, grad_rows(slice(i * PLEN, (i + 1) * PLEN), dkeys, dvalues))
        down_ref[...] = grad_rows(slice(remote, remote + tokens), dkeys, dvalues)


def attend(ids, queries, out_grad, query_kv, passage_kv, queries_here, retrieved, done=()):
    tokens = queries.shape[0] // queries_here
    width = query_kv.shape[1]
    heads = width // (2 * HD)
    wide = queries.shape[1] // heads
    group = wide // HD
    keys = retrieved * PLEN + tokens

    ready = 1 if done else 0

    def passage_spec(i):
        def where(h, n, ids):
            if ready:
                return ids[n * h * retrieved + i], 0, 0
            return ids[n * retrieved + i], 0, h

        return pl.BlockSpec((1, PLEN, 2 * HD), where)

    def done_row(h, n):
        return n * (1 - h) + (queries_here - 1) * h

    done_specs = [
        pl.BlockSpec((tokens, wide), lambda h, n, ids: (done_row(h, n), 0)),
        pl.BlockSpec((retrieved, PLEN, 2 * HD), lambda h, n, ids: (done_row(h, n), 0, 0)),
        pl.BlockSpec((tokens, 2 * HD), lambda h, n, ids: (done_row(h, n), 0)),
    ][: len(done)]
    wide_spec = pl.BlockSpec((tokens, wide), lambda h, n, ids: (n, h))
    own_spec = pl.BlockSpec((tokens, 2 * HD), lambda h, n, ids: (n, h))
    flops = 12 * queries_here * heads * group * tokens * keys * HD
    return pl.pallas_call(
        functools.partial(attend_kernel, group, retrieved, ready),
        grid_spec=pltpu.PrefetchScalarGridSpec(
            num_scalar_prefetch=1,
            grid=(heads, queries_here),
            in_specs=[wide_spec, wide_spec, own_spec] + done_specs + [passage_spec(i) for i in range(retrieved)],
            out_specs=[
                wide_spec,
                pl.BlockSpec((passage_kv.shape[0], PLEN, 2 * HD), lambda h, n, ids: (0, 0, h)),
                own_spec,
            ],
            scratch_shapes=[
                pltpu.VMEM((keys, HD), jnp.bfloat16),
                pltpu.VMEM((keys, HD), jnp.bfloat16),
                pltpu.VMEM((keys, HD), jnp.float32),
                pltpu.VMEM((keys, HD), jnp.float32),
            ],
        ),
        out_shape=[
            jax.ShapeDtypeStruct(queries.shape, jnp.bfloat16),
            jax.ShapeDtypeStruct((passage_kv.shape[0], PLEN, width), jnp.bfloat16),
            jax.ShapeDtypeStruct(query_kv.shape, jnp.bfloat16),
        ],
        compiler_params=pltpu.CompilerParams(vmem_limit_bytes=56 * MIB),
        cost_estimate=pl.CostEstimate(flops=flops, bytes_accessed=16 * MIB, transcendentals=0),
    )(ids, queries, out_grad, query_kv, *done, *([passage_kv] * retrieved))


def per_device(passage_hidden, kv_weight, queries, query_kv, out_grad, source_device, source_slot):
    owners = lax.axis_size("pas")
    shares = lax.axis_size("tp")
    share = lax.axis_index("tp")
    chips = owners // 2
    rows_local = passage_hidden.shape[0]
    local_width = query_kv.shape[1]
    passages_here = rows_local // PLEN
    queries_here, retrieved = source_device.shape
    projected = project(passage_hidden, kv_weight, chips, shares, 0)
    ids = (source_device * passages_here + source_slot).reshape(-1)
    heads = local_width // (2 * HD)
    if heads == 2 and chips <= 2 * queries_here and passages_here % 4 == 0:
        passage_kv, *done = early_attend(
            ids, queries, out_grad, query_kv, projected, chips, queries_here, retrieved, 1
        )
    else:
        passage_kv, done = ring_gather(projected, chips, 1), ()
        passage_kv = passage_kv.reshape(owners * passages_here, PLEN, local_width)
    grad_queries, dense, own_grads = attend(
        ids, queries, out_grad, query_kv, passage_kv, queries_here, retrieved, done
    )
    dense = dense.reshape(owners * rows_local, local_width)
    weight_grad = return_grads(dense, passage_hidden, chips, shares, kv_weight.shape[0], 2)
    return grad_queries, own_grads, weight_grad


def solution(mesh):
    in_specs = (
        P("pas", "tp"),
        P("pas", "tp"),
        P("pas", "tp"),
        P("pas", "tp"),
        P("pas", "tp"),
        P("pas", None),
        P("pas", None),
    )
    out_specs = (P("pas", "tp"), P("pas", "tp"), P("pas", "tp"))
    return jax.shard_map(
        per_device, mesh=mesh, in_specs=in_specs, out_specs=out_specs, check_vma=False
    )
```

```python
import functools
import math
import jax
import jax.numpy as jnp
from jax import lax
from jax.experimental import pallas as pl
from jax.experimental.pallas import tpu as pltpu
from jax.sharding import PartitionSpec as P

HD = 128
PLEN = 128
MIB = 1 << 20


def ring_place(chips):
    me = lax.axis_index("pas")
    core = lax.rem(me, 2)
    chip = lax.div(me, 2)
    side = lax.rem(chip, 2)
    deep = lax.div(chip, 2)
    place = deep + side * (chips - 1 - 2 * deep)

    def chip_at(position):
        q = lax.rem(position + 2 * chips, chips)
        half = lax.div(q, chips // 2)
        return 2 * q + half * (2 * chips - 1 - 4 * q)

    return core, place, chip_at


def greet(others, shares=()):
    barrier = pltpu.get_barrier_semaphore()
    for place in [{"pas": other} for other in others] + [{"tp": other} for other in shares]:
        pl.semaphore_signal(barrier, inc=1, device_id=place, device_id_type=pl.DeviceIdType.MESH)
    pl.semaphore_wait(barrier, len(others) + len(shares))


def send(src, dst, send_sem, recv_sem, other, axis="pas"):
    return pltpu.make_async_remote_copy(
        src_ref=src,
        dst_ref=dst,
        send_sem=send_sem,
        recv_sem=recv_sem,
        device_id={axis: other},
        device_id_type=pl.DeviceIdType.MESH,
    )


def gather_kernel(chips, lanes, x_ref, out_ref, own_sem, ring_send, ring_recv, pair_send, pair_recv):
    core, place, chip_at = ring_place(chips)
    mine = chip_at(place)
    partner = 2 * mine + 1 - core
    nexts = (2 * chip_at(place + 1) + core, 2 * chip_at(place - 1) + core)
    greet((nexts[0], nexts[1], partner))
    rings, pairs = {}, []
    for step in range(chips):
        for lane in range(lanes):
            for way in range(2):
                back = step if way == 0 else -step
                where = chip_at(place - back)
                slot = out_ref.at[where, core, way, lane]
                if step == 0:
                    src = x_ref.at[way, lane]
                else:
                    rings[step - 1, way, lane].wait_recv()
                    src = slot
                if step < chips - 1:
                    copy = send(
                        src, slot, ring_send.at[step, way, lane], ring_recv.at[step, way, lane], nexts[way]
                    )
                    copy.start()
                    rings[step, way, lane] = copy
                copy = send(
                    src, slot, pair_send.at[step, way, lane], pair_recv.at[step, way, lane], partner
                )
                copy.start()
                pairs.append(copy)
        if step == 0:
            own = pltpu.make_async_copy(x_ref, out_ref.at[mine, core], own_sem)
            own.start()
    own.wait()
    for copy in rings.values():
        copy.wait_send()
    for copy in pairs:
        copy.wait()


def ring_gather(x, chips, collective_id):
    rows, width = x.shape
    lanes = 2 if rows % 64 == 0 else 1
    high = rows // (2 * lanes)
    out = pl.pallas_call(
        functools.partial(gather_kernel, chips, lanes),
        out_shape=jax.ShapeDtypeStruct((chips, 2, 2, lanes, high, width), x.dtype),
        in_specs=[pl.BlockSpec(memory_space=pl.ANY)],
        out_specs=pl.BlockSpec(memory_space=pl.ANY),
        scratch_shapes=[
            pltpu.SemaphoreType.DMA,
            pltpu.SemaphoreType.DMA((chips, 2, lanes)),
            pltpu.SemaphoreType.DMA((chips, 2, lanes)),
            pltpu.SemaphoreType.DMA((chips, 2, lanes)),
            pltpu.SemaphoreType.DMA((chips, 2, lanes)),
        ],
        compiler_params=pltpu.CompilerParams(collective_id=collective_id, has_side_effects=True),
    )(x.reshape(2, lanes, high, width))
    return out.reshape(chips * 2 * rows, width)


def project_kernel(
    chips, shares, lanes, hidden_ref, x_ref, out_ref, hidden, weight, joined, part, got,
    own_sem, hidden_sem, ring_send, ring_recv, pair_send, pair_recv, share_send, share_recv,
):
    core, place, chip_at = ring_place(chips)
    share = lax.axis_index("tp")
    mine = chip_at(place)
    partner = 2 * mine + 1 - core
    nexts = (2 * chip_at(place + 1) + core, 2 * chip_at(place - 1) + core)
    load = pltpu.make_async_copy(hidden_ref, hidden, hidden_sem)
    load.start()
    own = pltpu.make_async_copy(x_ref, weight.at[mine, core], own_sem)
    own.start()
    greet(
        (nexts[0], nexts[1], partner),
        [lax.rem(share + k, shares) for k in range(1, shares)],
    )
    rows = hidden.shape[0]
    tile = min(256, rows)
    half = part.shape[2]
    each = half // 2
    group = chips // shares
    rings, pairs = {}, {}

    def chip_of(step, way):
        return chip_at(place - step if way == 0 else place + step)

    def goal(step, way):
        return lax.div(chip_of(step, way), group)

    def share_copy(step, way):
        target = goal(step, way)
        slot = lax.rem(target - share + 2 * shares - 1, shares)
        slot = lax.rem(slot, shares - 1)
        return send(
            part.at[way, step],
            got.at[slot, way, step],
            share_send.at[way, step],
            share_recv.at[slot, way, step],
            target,
            "tp",
        )

    def multiply(step):
        for way in range(2):
            for lane in range(lanes):
                pairs[step, way, lane].wait_recv()
            piece = weight[chip_of(step, way), :, way]
            joined[way * half : (way + 1) * half, :] = piece.reshape(half, piece.shape[-1])

        def one(index, carry):
            here = pl.ds(pl.multiple_of(index * tile, tile), tile)
            product = lax.dot_general(
                joined[...], hidden[here, :], (((1,), (1,)), ((), ())),
                preferred_element_type=jnp.float32,
            )
            part[0, step, :, here] = product[:half]
            part[1, step, :, here] = product[half:]
            return carry

        lax.fori_loop(0, rows // tile, one, 0)
        for way in range(2):

            @pl.when(goal(step, way) != share)
            def _(way=way):
                share_copy(step, way).start()

    for step in range(chips):
        for lane in range(lanes):
            for way in range(2):
                slot = weight.at[chip_of(step, way), core, way, lane]
                if step == 0:
                    src = x_ref.at[way, lane]
                else:
                    rings[step - 1, way, lane].wait_recv()
                    src = slot
                if step < chips - 1:
                    copy = send(
                        src, slot, ring_send.at[step, way, lane], ring_recv.at[step, way, lane], nexts[way]
                    )
                    copy.start()
                    rings[step, way, lane] = copy
                copy = send(
                    src, slot, pair_send.at[step, way, lane], pair_recv.at[step, way, lane], partner
                )
                copy.start()
                pairs[step, way, lane] = copy
        if step == 0:
            load.wait()
            own.wait()
        else:
            multiply(step - 1)
    multiply(chips - 1)
    for step in range(chips):
        for way in range(2):

            @pl.when(goal(step, way) == share)
            def _(step=step, way=way):
                total = part[way, step]
                for slot in range(shares - 1):
                    send(
                        part.at[way, step],
                        got.at[slot, way, step],
                        share_send.at[way, step],
                        share_recv.at[slot, way, step],
                        lax.rem(share + 1, shares),
                        "tp",
                    ).wait_recv()
                    total = total + got[slot, way, step]
                total = total.astype(out_ref.dtype)
                where = lax.rem(chip_of(step, way), group)
                out_ref[where, 0, way] = total[:each]
                out_ref[where, 1, way] = total[each:]

            @pl.when(goal(step, way) != share)
            def _(step=step, way=way):
                share_copy(step, way).wait_send()

    for copy in rings.values():
        copy.wait_send()
    for copy in pairs.values():
        copy.wait_send()


def project(hidden, kv_weight, chips, shares, collective_id):
    rows, width = hidden.shape
    high = kv_weight.shape[0]
    lanes = 2 if high % 64 == 0 else 1
    high = high // (2 * lanes)
    half = 2 * lanes * high
    group = chips // shares
    step_sems = pltpu.SemaphoreType.DMA((chips, 2, lanes))
    out = pl.pallas_call(
        functools.partial(project_kernel, chips, shares, lanes),
        out_shape=jax.ShapeDtypeStruct((group, 2, 2, lanes * high, rows), jnp.bfloat16),
        in_specs=[pl.BlockSpec(memory_space=pl.ANY)] * 2,
        out_specs=pl.BlockSpec(memory_space=pltpu.VMEM),
        scratch_shapes=[
            pltpu.VMEM((rows, width), hidden.dtype),
            pltpu.VMEM((chips, 2, 2, lanes, high, width), kv_weight.dtype),
            pltpu.VMEM((2 * half, width), kv_weight.dtype),
            pltpu.VMEM((2, chips, half, rows), jnp.float32),
            pltpu.VMEM((shares - 1, 2, chips, half, rows), jnp.float32),
            pltpu.SemaphoreType.DMA,
            pltpu.SemaphoreType.DMA,
            step_sems,
            step_sems,
            step_sems,
            step_sems,
            pltpu.SemaphoreType.DMA((2, chips)),
            pltpu.SemaphoreType.DMA((shares - 1, 2, chips)),
        ],
        compiler_params=pltpu.CompilerParams(
            collective_id=collective_id, has_side_effects=True, vmem_limit_bytes=56 * MIB
        ),
    )(hidden, kv_weight.reshape(2, lanes, high, width))
    return out.reshape(group * 2 * 2 * lanes * high, rows).T


def return_kernel(
    chips, shares, lanes, thin, x_ref, hidden_ref, out_ref,
    mine, pair, got, full, hidden, joined, ours, theirs, pair_low, got_low,
    hidden_sem, own_sem, pair_send, pair_recv, ring_send, ring_recv, share_send, share_recv,
    low_pair_send, low_pair_recv, low_ring_send, low_ring_recv,
):
    core, place, chip_at = ring_place(chips)
    share = lax.axis_index("tp")
    partner = 2 * chip_at(place) + 1 - core
    nexts = (2 * chip_at(place + 1) + core, 2 * chip_at(place - 1) + core)
    heads, _, _, _, high, wide = mine.shape
    rows, width = hidden.shape
    local = heads * wide
    load = pltpu.make_async_copy(hidden_ref, hidden, hidden_sem)
    owns, pairs, rings, sent = {}, {}, {}, []
    greet(
        (nexts[0], nexts[1], partner),
        [lax.rem(share + k, shares) for k in range(1, shares)],
    )

    def chip_of(step, way):
        return chip_at(place - 1 - step if way == 0 else place + 1 + step)

    for head in range(heads):
        columns = pl.ds(head * wide, wide)
        for step in range(chips):
            for way in range(2):
                where = chip_of(step, way)
                copy = send(
                    x_ref.at[where, 1 - core, way, :, :, columns],
                    pair.at[head, way, step],
                    pair_send.at[head, way, step],
                    pair_recv.at[head, way, step],
                    partner,
                )
                copy.start()
                pairs[head, way, step] = copy
                sent.append(copy)
                copy = pltpu.make_async_copy(
                    x_ref.at[where, core, way, :, :, columns],
                    mine.at[head, way, step],
                    own_sem.at[head, way, step],
                )
                copy.start()
                owns[head, way, step] = copy
    load.start()

    def share_copy(head, origin, k):
        slot = full.at[pl.ds(pl.multiple_of(origin * local + head * wide, wide), wide)]
        return send(
            slot, slot, share_send.at[head, k - 1], share_recv.at[head, k - 1],
            lax.rem(share + k, shares), "tp",
        )

    def work(head, step):
        last = step == chips - 1
        for lane in range(lanes):
            for way in range(2):
                if lane == 0:
                    owns[head, way, step].wait()
                    pairs[head, way, step].wait_recv()
                if step > 0:
                    rings[head, step - 1, way, lane].wait_recv()
                if last:
                    total = mine[head, way, step, lane].astype(jnp.float32)
                    total += pair[head, way, step, lane].astype(jnp.float32)
                    total += got[head, way, step - 1, lane].astype(jnp.float32)
                    start = pl.multiple_of(share * local + head * wide, wide)
                    there = (way * lanes + lane) * high
                    full[pl.ds(start, wide), there : there + high] = total.T.astype(full.dtype)
                    continue

                def add(index, carry, way=way, lane=lane):
                    here = pl.ds(pl.multiple_of(index * 32, 32), 32)
                    total = mine[head, way, step, lane, here, :].astype(jnp.float32)
                    total += pair[head, way, step, lane, here, :].astype(jnp.float32)
                    if step > 0:
                        total += got[head, way, step - 1, lane, here, :].astype(jnp.float32)
                    mine[head, way, step, lane, here, :] = total.astype(mine.dtype)
                    return carry

                lax.fori_loop(0, high // 32, add, 0)
                copy = send(
                    mine.at[head, way, step, lane],
                    got.at[head, way, step, lane],
                    ring_send.at[head, step, way, lane],
                    ring_recv.at[head, step, way, lane],
                    nexts[way],
                )
                copy.start()
                rings[head, step, way, lane] = copy
                sent.append(copy)
        if last:
            for k in range(1, shares):
                copy = share_copy(head, share, k)
                copy.start()
                sent.append(copy)

    for head in range(heads):
        for step in range(chips):
            if step == chips - 1 and head + 1 < heads:
                work(head + 1, 0)
            if step == 0 and head > 0:
                continue
            work(head, step)
    load.wait()
    for head in range(heads):
        for k in range(1, shares):
            share_copy(head, lax.rem(share + shares - k, shares), k).wait_recv()

    each = joined.shape[0] // 4
    short = each // thin
    tile = min(512, width)
    low_pairs, low_rings = {}, {}

    def multiply(step):
        for way in range(2):
            for other in range(2):
                side = core if other == 0 else 1 - core
                start = ((2 * chip_of(step, way) + side) * 2 + way) * each
                there = (2 * way + other) * each
                joined[there : there + each, :] = full[pl.ds(pl.multiple_of(start, each), each), :]

        def one(index, carry):
            here = pl.ds(pl.multiple_of(index * tile, tile), tile)
            product = jnp.dot(
                joined[...], hidden[:, here], preferred_element_type=jnp.float32
            ).astype(ours.dtype)
            for way in range(2):
                there = 2 * way * each
                ours[way, step, :, here] = product[there : there + each]
                theirs[way, step, :, here] = product[there + each : there + 2 * each]
            return carry

        lax.fori_loop(0, width // tile, one, 0)
        for way in range(2):
            copy = send(
                theirs.at[way, step],
                pair_low.at[way, step],
                low_pair_send.at[way, step],
                low_pair_recv.at[way, step],
                partner,
            )
            copy.start()
            low_pairs[way, step] = copy
            sent.append(copy)

    def pass_on(step):
        last = step == chips - 1
        for lane in range(thin):
            for way in range(2):
                if lane == 0:
                    low_pairs[way, step].wait_recv()
                if step > 0:
                    low_rings[step - 1, way, lane].wait_recv()
                here = slice(lane * short, (lane + 1) * short)

                def add(index, carry, way=way, here=here):
                    there = pl.ds(pl.multiple_of(index * tile, tile), tile)
                    total = ours[way, step, here, there].astype(jnp.float32)
                    total += pair_low[way, step, here, there].astype(jnp.float32)
                    if step > 0:
                        total += got_low[way, step - 1, here, there].astype(jnp.float32)
                    if last:
                        out_ref[way, here, there] = total
                    else:
                        ours[way, step, here, there] = total.astype(ours.dtype)
                    return carry

                lax.fori_loop(0, width // tile, add, 0)
                if not last:
                    copy = send(
                        ours.at[way, step, here],
                        got_low.at[way, step, here],
                        low_ring_send.at[step, way, lane],
                        low_ring_recv.at[step, way, lane],
                        nexts[way],
                    )
                    copy.start()
                    low_rings[step, way, lane] = copy
                    sent.append(copy)

    multiply(0)
    for step in range(chips):
        if step + 1 < chips:
            multiply(step + 1)
        pass_on(step)
    for copy in sent:
        copy.wait_send()


def return_grads(dense, hidden, chips, shares, out_rows, collective_id):
    rows, width = hidden.shape
    local = dense.shape[1]
    wide = 2 * HD
    heads = local // wide
    lanes = 4 if rows % 512 == 0 else 2
    high = rows // (2 * lanes)
    each = out_rows // 2
    thin = 2 if each % 32 == 0 else 1
    slots = pltpu.VMEM((heads, 2, chips, lanes, high, wide), dense.dtype)
    low_slots = pltpu.VMEM((2, chips, each, width), dense.dtype)
    head_sems = pltpu.SemaphoreType.DMA((heads, 2, chips))
    lane_sems = pltpu.SemaphoreType.DMA((heads, chips, 2, lanes))
    share_sems = pltpu.SemaphoreType.DMA((heads, shares - 1))
    low_sems = pltpu.SemaphoreType.DMA((2, chips))
    thin_sems = pltpu.SemaphoreType.DMA((chips, 2, thin))
    out = pl.pallas_call(
        functools.partial(return_kernel, chips, shares, lanes, thin),
        out_shape=jax.ShapeDtypeStruct((2, each, width), jnp.float32),
        in_specs=[pl.BlockSpec(memory_space=pl.ANY)] * 2,
        out_specs=pl.BlockSpec(memory_space=pltpu.VMEM),
        scratch_shapes=[
            slots, slots, slots,
            pltpu.VMEM((shares * local, rows), dense.dtype),
            pltpu.VMEM((rows, width), hidden.dtype),
            pltpu.VMEM((4 * each, rows), dense.dtype),
            low_slots, low_slots, low_slots, low_slots,
            pltpu.SemaphoreType.DMA,
            head_sems, head_sems, head_sems,
            lane_sems, lane_sems,
            share_sems, share_sems,
            low_sems, low_sems,
            thin_sems, thin_sems,
        ],
        compiler_params=pltpu.CompilerParams(
            collective_id=collective_id, has_side_effects=True, vmem_limit_bytes=60 * MIB
        ),
    )(dense.reshape(chips, 2, 2, lanes, high, local), hidden)
    return out.reshape(out_rows, width)


def attend_rows(
    group, retrieved, rows, passage, q_ref, g_ref, own_ref, dq_ref, keys, values, dkeys, dvalues, between
):
    scaling = HD ** (-0.5)
    remote = retrieved * PLEN
    tokens = keys.shape[0] - remote
    for i in range(retrieved):
        block = passage(i)
        keys[i * PLEN : (i + 1) * PLEN, :] = block[:, :HD]
        values[i * PLEN : (i + 1) * PLEN, :] = block[:, HD:]
    keys[remote:, :] = own_ref[rows, :HD]
    values[remote:, :] = own_ref[rows, HD:]
    row = lax.broadcasted_iota(jnp.int32, (2 * tokens, tokens), 0)
    col = lax.broadcasted_iota(jnp.int32, (2 * tokens, tokens), 1)
    hidden = col > jnp.where(row >= tokens, row - tokens, row)

    def dot(a, b, dims):
        return lax.dot_general(a, b, ((dims[0], dims[1]), ((), ())), preferred_element_type=jnp.float32)

    for pair in range(group // 2):
        lo, mid, hi = 2 * pair * HD, (2 * pair + 1) * HD, (2 * pair + 2) * HD
        q = jnp.concatenate([q_ref[rows, lo:mid], q_ref[rows, mid:hi]], axis=0)
        g = jnp.concatenate([g_ref[rows, lo:mid], g_ref[rows, mid:hi]], axis=0)
        k, v = keys[...], values[...]
        scores = dot(q, k, ((1,), (1,)))
        tail = jnp.where(hidden, jnp.float32(-1e30), scores[:, remote:])
        scores = jnp.concatenate([scores[:, :remote], tail], axis=1)
        largest = jnp.max(scores, axis=1, keepdims=True)
        exponent = jnp.exp2((scores - largest) * jnp.float32(scaling * math.log2(math.e)))
        weights = exponent * (1.0 / jnp.sum(exponent, axis=1, keepdims=True))
        low = weights.astype(jnp.bfloat16)
        outputs = dot(low, v, ((1,), (0,)))
        delta = jnp.sum(outputs * g.astype(jnp.float32), axis=1, keepdims=True)
        grad = (weights * (dot(g, v, ((1,), (1,))) - delta)).astype(jnp.bfloat16)
        dq = (dot(grad, k, ((1,), (0,))) * scaling).astype(dq_ref.dtype)
        dq_ref[rows, lo:mid] = dq[:tokens]
        dq_ref[rows, mid:hi] = dq[tokens:]
        dk = dot(grad, q, ((0,), (0,)))
        dv = dot(low, g, ((0,), (0,)))
        if pair == 0:
            dkeys[...] = dk
            dvalues[...] = dv
        else:
            dkeys[...] += dk
            dvalues[...] += dv
        between(pair)


def grad_rows(rows, dkeys, dvalues):
    scaling = HD ** (-0.5)
    both = jnp.concatenate([dkeys[rows, :] * scaling, dvalues[rows, :]], axis=1)
    return both.astype(jnp.bfloat16)


def early_kernel(
    chips, group, retrieved, ids_ref, x_ref, q_ref, g_ref, own_ref,
    late_ref, dq_ref, remote_ref, down_ref, early, keys, values, dkeys, dvalues,
    own_sem, ring_send, ring_recv, pair_send, pair_recv,
):
    core, place, chip_at = ring_place(chips)
    mine = chip_at(place)
    partner = 2 * mine + 1 - core
    nexts = (2 * chip_at(place + 1) + core, 2 * chip_at(place - 1) + core)
    here = x_ref.shape[0]
    per = here // 4
    wide = 2 * HD
    remote = retrieved * PLEN
    tokens = keys.shape[0] - remote
    targets = (early, late_ref)

    def first(step, way, lane, side):
        where = chip_at(place - step if way == 0 else place + step)
        return (2 * where + side) * here + (2 * way + lane) * per

    def block(head, step, way, lane):
        return targets[head].at[pl.ds(first(step, way, lane, core), per)]

    def source(head, way, lane):
        return x_ref.at[pl.ds((2 * way + lane) * per, per), :, pl.ds(head * wide, wide)]

    def ring_copy(head, step, way, lane, src):
        return send(
            src, block(head, step, way, lane),
            ring_send.at[head, step, way, lane], ring_recv.at[head, step, way, lane], nexts[way],
        )

    def pair_copy(head, step, way, lane, src):
        return send(
            src, block(head, step, way, lane),
            pair_send.at[head, step, way, lane], pair_recv.at[head, step, way, lane], partner,
        )

    def own_copy(head):
        return pltpu.make_async_copy(
            x_ref.at[:, :, pl.ds(head * wide, wide)],
            targets[head].at[pl.ds((2 * mine + core) * here, here)],
            own_sem.at[head],
        )

    def begin(head):
        for lane in range(2):
            for way in range(2):
                ring_copy(head, 0, way, lane, source(head, way, lane)).start()
                pair_copy(head, 0, way, lane, source(head, way, lane)).start()
        own_copy(head).start()

    def serve(head, step):
        for lane in range(2):
            for way in range(2):
                slot = block(head, step, way, lane)
                ring_copy(head, step - 1, way, lane, slot).wait_recv()

                @pl.when(step < chips - 1)
                def _(way=way, lane=lane, slot=slot):
                    ring_copy(head, step, way, lane, slot).start()

                pair_copy(head, step, way, lane, slot).start()

    def finish_pairs(head):
        def one(step, carry):
            for lane in range(2):
                for way in range(2):
                    pair_copy(head, step, way, lane, block(head, step, way, lane)).wait_recv()
            return carry

        lax.fori_loop(0, chips, one, 0)
        own_copy(head).wait()

    greet((nexts[0], nexts[1], partner))
    begin(0)

    def steps(step, carry):
        serve(0, step)
        return carry

    lax.fori_loop(1, chips - 1, steps, 0)
    begin(1)
    serve(0, chips - 1)
    finish_pairs(0)

    def one_query(query, carry):
        rows = pl.ds(pl.multiple_of(query * tokens, tokens), tokens)

        def between(pair):
            if pair % 2 == 1 and pair < 4:
                step = 2 * query + 1 + pair // 2

                @pl.when(step < chips)
                def _():
                    serve(1, step)

        attend_rows(
            group, retrieved, rows, lambda i: early[ids_ref[query * retrieved + i]],
            q_ref, g_ref, own_ref, dq_ref, keys, values, dkeys, dvalues, between,
        )
        for i in range(retrieved):
            remote_ref[query * retrieved + i] = grad_rows(
                slice(i * PLEN, (i + 1) * PLEN), dkeys, dvalues
            )
        down_ref[rows, :] = grad_rows(slice(remote, remote + tokens), dkeys, dvalues)
        return carry

    lax.fori_loop(0, q_ref.shape[0] // tokens, one_query, 0)
    finish_pairs(1)

    def sent(step, carry):
        for head in range(2):
            for lane in range(2):
                for way in range(2):
                    slot = block(head, step, way, lane)
                    pair_copy(head, step, way, lane, slot).wait_send()

                    @pl.when(step < chips - 1)
                    def _(head=head, way=way, lane=lane, slot=slot):
                        ring_copy(head, step, way, lane, slot).wait_send()

        return carry

    lax.fori_loop(0, chips, sent, 0)


def early_attend(ids, queries, out_grad, query_kv, projected, chips, queries_here, retrieved, collective_id):
    rows, _ = projected.shape
    here = rows // PLEN
    total = 2 * chips * here
    wide = 2 * HD
    heads = query_kv.shape[1] // wide
    broad = queries.shape[1] // heads
    tokens = queries.shape[0] // queries_here
    keys = retrieved * PLEN + tokens
    sems = pltpu.SemaphoreType.DMA((2, chips, 2, 2))
    return pl.pallas_call(
        functools.partial(early_kernel, chips, broad // HD, retrieved),
        grid=(1,),
        out_shape=[
            jax.ShapeDtypeStruct((total, PLEN, wide), jnp.bfloat16),
            jax.ShapeDtypeStruct((queries.shape[0], broad), jnp.bfloat16),
            jax.ShapeDtypeStruct((queries_here * retrieved, PLEN, wide), jnp.bfloat16),
            jax.ShapeDtypeStruct((queries.shape[0], wide), jnp.bfloat16),
        ],
        in_specs=[
            pl.BlockSpec(memory_space=pltpu.SMEM),
            pl.BlockSpec(memory_space=pl.ANY),
            pl.BlockSpec((queries.shape[0], broad), lambda i: (0, 0)),
            pl.BlockSpec((queries.shape[0], broad), lambda i: (0, 0)),
            pl.BlockSpec((queries.shape[0], wide), lambda i: (0, 0)),
        ],
        out_specs=[
            pl.BlockSpec(memory_space=pl.ANY),
            pl.BlockSpec((queries.shape[0], broad), lambda i: (0, 0)),
            pl.BlockSpec((queries_here * retrieved, PLEN, wide), lambda i: (0, 0, 0)),
            pl.BlockSpec((queries.shape[0], wide), lambda i: (0, 0)),
        ],
        scratch_shapes=[
            pltpu.VMEM((total, PLEN, wide), jnp.bfloat16),
            pltpu.VMEM((keys, HD), jnp.bfloat16),
            pltpu.VMEM((keys, HD), jnp.bfloat16),
            pltpu.VMEM((keys, HD), jnp.float32),
            pltpu.VMEM((keys, HD), jnp.float32),
            pltpu.SemaphoreType.DMA((2,)),
            sems, sems, sems, sems,
        ],
        compiler_params=pltpu.CompilerParams(
            collective_id=collective_id, has_side_effects=True, vmem_limit_bytes=56 * MIB
        ),
    )(ids, projected.reshape(here, PLEN, -1), queries, out_grad, query_kv)


def attend_kernel(group, retrieved, ready, ids_ref, q_ref, g_ref, own_ref, *refs):
    done, refs = refs[: 3 * ready], refs[3 * ready :]
    passages = refs[:retrieved]
    dq_ref, dense_ref, down_ref, keys, values, dkeys, dvalues = refs[retrieved:]
    remote = retrieved * PLEN
    tokens = q_ref.shape[0]
    head, query = pl.program_id(0), pl.program_id(1)

    @pl.when(query == 0)
    def _():
        def clear(p, carry):
            dense_ref[p] = jnp.zeros(dense_ref.shape[1:], dense_ref.dtype)
            return carry

        lax.fori_loop(0, dense_ref.shape[0], clear, 0)

    def place(i, block):
        p = ids_ref[query * retrieved + i]
        total = dense_ref[p].astype(jnp.float32) + block.astype(jnp.float32)
        dense_ref[p] = total.astype(dense_ref.dtype)

    if ready:

        @pl.when(head == 0)
        def _():
            for i in range(retrieved):
                place(i, done[1][i])
            dq_ref[...] = done[0][...]
            down_ref[...] = done[2][...]

    @pl.when(head >= ready)
    def _():
        attend_rows(
            group, retrieved, slice(0, tokens), lambda i: passages[i][0],
            q_ref, g_ref, own_ref, dq_ref, keys, values, dkeys, dvalues, lambda pair: None,
        )
        for i in range(retrieved):
            place(i, grad_rows(slice(i * PLEN, (i + 1) * PLEN), dkeys, dvalues))
        down_ref[...] = grad_rows(slice(remote, remote + tokens), dkeys, dvalues)


def attend(ids, queries, out_grad, query_kv, passage_kv, queries_here, retrieved, done=()):
    tokens = queries.shape[0] // queries_here
    width = query_kv.shape[1]
    heads = width // (2 * HD)
    wide = queries.shape[1] // heads
    group = wide // HD
    keys = retrieved * PLEN + tokens

    ready = 1 if done else 0

    def passage_spec(i):
        def where(h, n, ids):
            if ready:
                return ids[n * h * retrieved + i], 0, 0
            return ids[n * retrieved + i], 0, h

        return pl.BlockSpec((1, PLEN, 2 * HD), where)

    def done_row(h, n):
        return n * (1 - h) + (queries_here - 1) * h

    done_specs = [
        pl.BlockSpec((tokens, wide), lambda h, n, ids: (done_row(h, n), 0)),
        pl.BlockSpec((retrieved, PLEN, 2 * HD), lambda h, n, ids: (done_row(h, n), 0, 0)),
        pl.BlockSpec((tokens, 2 * HD), lambda h, n, ids: (done_row(h, n), 0)),
    ][: len(done)]
    wide_spec = pl.BlockSpec((tokens, wide), lambda h, n, ids: (n, h))
    own_spec = pl.BlockSpec((tokens, 2 * HD), lambda h, n, ids: (n, h))
    flops = 12 * queries_here * heads * group * tokens * keys * HD
    return pl.pallas_call(
        functools.partial(attend_kernel, group, retrieved, ready),
        grid_spec=pltpu.PrefetchScalarGridSpec(
            num_scalar_prefetch=1,
            grid=(heads, queries_here),
            in_specs=[wide_spec, wide_spec, own_spec] + done_specs + [passage_spec(i) for i in range(retrieved)],
            out_specs=[
                wide_spec,
                pl.BlockSpec((passage_kv.shape[0], PLEN, 2 * HD), lambda h, n, ids: (0, 0, h)),
                own_spec,
            ],
            scratch_shapes=[
                pltpu.VMEM((keys, HD), jnp.bfloat16),
                pltpu.VMEM((keys, HD), jnp.bfloat16),
                pltpu.VMEM((keys, HD), jnp.float32),
                pltpu.VMEM((keys, HD), jnp.float32),
            ],
        ),
        out_shape=[
            jax.ShapeDtypeStruct(queries.shape, jnp.bfloat16),
            jax.ShapeDtypeStruct((passage_kv.shape[0], PLEN, width), jnp.bfloat16),
            jax.ShapeDtypeStruct(query_kv.shape, jnp.bfloat16),
        ],
        compiler_params=pltpu.CompilerParams(vmem_limit_bytes=56 * MIB),
        cost_estimate=pl.CostEstimate(flops=flops, bytes_accessed=16 * MIB, transcendentals=0),
    )(ids, queries, out_grad, query_kv, *done, *([passage_kv] * retrieved))


def per_device(passage_hidden, kv_weight, queries, query_kv, out_grad, source_device, source_slot):
    owners = lax.axis_size("pas")
    shares = lax.axis_size("tp")
    share = lax.axis_index("tp")
    chips = owners // 2
    rows_local = passage_hidden.shape[0]
    local_width = query_kv.shape[1]
    passages_here = rows_local // PLEN
    queries_here, retrieved = source_device.shape
    projected = project(passage_hidden, kv_weight, chips, shares, 0)
    ids = (source_device * passages_here + source_slot).reshape(-1)
    heads = local_width // (2 * HD)
    if heads == 2 and chips <= 2 * queries_here and passages_here % 4 == 0:
        passage_kv, *done = early_attend(
            ids, queries, out_grad, query_kv, projected, chips, queries_here, retrieved, 1
        )
    else:
        passage_kv, done = ring_gather(projected, chips, 1), ()
        passage_kv = passage_kv.reshape(owners * passages_here, PLEN, local_width)
    grad_queries, dense, own_grads = attend(
        ids, queries, out_grad, query_kv, passage_kv, queries_here, retrieved, done
    )
    dense = dense.reshape(owners * rows_local, local_width)
    weight_grad = return_grads(dense, passage_hidden, chips, shares, kv_weight.shape[0], 2)
    return grad_queries, own_grads, weight_grad


def solution(mesh):
    in_specs = (
        P("pas", "tp"),
        P("pas", "tp"),
        P("pas", "tp"),
        P("pas", "tp"),
        P("pas", "tp"),
        P("pas", None),
        P("pas", None),
    )
    out_specs = (P("pas", "tp"), P("pas", "tp"), P("pas", "tp"))
    return jax.shard_map(
        per_device, mesh=mesh, in_specs=in_specs, out_specs=out_specs, check_vma=False
    )
```
